32 devices in a mesh: ctx: 8 (over z, core), chan: 4 (over y, x).
Axes of the slice: x: 2, y: 2, z: 4, core: 2. Of those that a mesh axis runs over, the one named last changes fastest.
Arguments:
- key_stream: bfloat16 [2048, 8192], P('ctx', 'chan'), may hold values from -6 to 6
- value_stream: bfloat16 [2048, 8192], P('ctx', 'chan'), may hold values from -6 to 6
- query_stream: bfloat16 [2048, 8192], P('ctx', 'chan'), may hold values from -6 to 6
- grad_out: bfloat16 [2048, 8192], P('ctx', 'chan'), may hold values from -6 to 6
- distant_lag_taps: bfloat16 [16, 2, 512], replicated, may hold values from -0.21875 to 0.21875
- near_taps: bfloat16 [16, 256], replicated, may hold values from -0.21875 to 0.21875
- lag_blocks: int32 [16, 2], replicated, may hold values from 1 to 3, as said below
Outputs:
- block_out: bfloat16 [2048, 8192], P('ctx', 'chan')
- grad_values: bfloat16 [2048, 8192], P('ctx', 'chan')
- grad_far: float32 [16, 2, 512], replicated
- grad_near: float32 [16, 256], replicated
The draws below stay inside these ranges and needn't reach their ends.
Inputs may be any that keep to these rules, and one draw needn't show every extreme that they name: `lag_blocks`: the lags of one group are distinct, and every group lists the lag block 3.
All inputs are finite; a program needn't handle non-finite values.
Results may differ from the reference program's by a relative error of at most 0.0049.
Values may be sent and summed in bfloat16 or wider, within the bound.
No kernel may reach another device: no remote copies, remote signals or barrier semaphores. Data moves between devices by JAX's collectives and lax.ppermute only.
A program may use at most 128 MiB of HBM per device.

```python
import math
import jax
import jax.numpy as jnp
from jax import lax

D = 8192
GSIZE = 512
WIN = 4
KB = 2
TOK_DEV = 256
G = 16
TOKENS = 2048
N_CTX = 8


def draw_lag_blocks(key, part):
    group_keys = jax.random.split(jax.random.fold_in(key, 17), G)

    def one_group(group_key):
        first_key, second_key = jax.random.split(group_key)
        others = jax.random.permutation(first_key, jnp.arange(1, WIN - 1, dtype=jnp.int32))[:KB - 1]
        listed = jnp.concatenate([others, jnp.full((1,), WIN - 1, jnp.int32)])
        ordering = jax.random.permutation(second_key, KB)
        return listed[ordering]
    return jax.vmap(one_group)(group_keys).astype(jnp.int32)


def block_levels(own_key, extent, cuts, low, largest):
    level = 1.0
    for axis_at, blocks in cuts:
        steps = jax.random.uniform(jax.random.fold_in(jax.random.fold_in(own_key, 6), axis_at), (blocks,), jnp.float32, low / len(cuts), largest / len(cuts))
        level = level * jnp.repeat(jnp.exp(steps), extent[axis_at] // blocks).reshape((-1,) + (1,) * (len(extent) - 1 - axis_at))
    return level


def noise(own_key, extent, scale, most, shards=(), kind=jnp.bfloat16):
    array = scale * jax.random.normal(own_key, extent, jnp.float32)
    if shards:
        array = array * block_levels(own_key, extent, shards, -0.22, 0.18)
    return jnp.clip(array, -most, most).astype(kind)


def setup_inputs(seed: int = 0) -> dict:
    key_of = jax.random.split(jax.random.key(seed), 8)
    return {
        "key_stream": noise(key_of[0], (TOKENS, D), 1.0, 6.0, ((0, 8), (1, 4))),
        "value_stream": noise(key_of[1], (TOKENS, D), 1.0, 6.0, ((0, 8), (1, 4))),
        "query_stream": noise(key_of[2], (TOKENS, D), 1.0, 6.0, ((0, 8), (1, 4))),
        "grad_out": noise(key_of[3], (TOKENS, D), 1.0, 6.0, ((0, 8), (1, 4))),
        "distant_lag_taps": noise(key_of[4], (G, KB, 2 * TOK_DEV), (TOK_DEV * (KB + 1)) ** -0.5, 0.21875),
        "near_taps": noise(key_of[5], (G, TOK_DEV), (TOK_DEV * (KB + 1)) ** -0.5, 0.21875),
        "lag_blocks": draw_lag_blocks(jax.random.fold_in(key_of[7], 71), 0),
    }


def toeplitz_matrix(tap_vector, span_len):
    target_pos = jnp.arange(span_len).astype(jnp.int32)[:, None]
    source_pos = jnp.arange(span_len).astype(jnp.int32)[None, :]
    return tap_vector[target_pos - source_pos + span_len]

def diagonal_totals(matrix, span_len):
    target_pos = jnp.arange(span_len).astype(jnp.int32)[:, None]
    source_pos = jnp.arange(span_len).astype(jnp.int32)[None, :]
    index_map = target_pos - source_pos + span_len
    return jnp.zeros((2 * span_len,), jnp.float32).at[index_map].add(matrix)

def reference(key_stream, value_stream, query_stream, grad_out, distant_lag_taps, near_taps, lag_blocks):
    span_len = TOK_DEV
    span_count = N_CTX
    nblocks = D // 128
    mixed = (key_stream.astype(jnp.float32) * value_stream.astype(jnp.float32)).astype(jnp.bfloat16)
    mixed = lax.optimization_barrier(mixed).astype(jnp.float32)
    gated = (grad_out.astype(jnp.float32) * query_stream.astype(jnp.float32)).astype(jnp.bfloat16)
    gated = lax.optimization_barrier(gated).astype(jnp.float32)
    input_block_rows = mixed.reshape(span_count, span_len, nblocks, 128).transpose(2, 0, 1, 3)
    grad_blocks = gated.reshape(span_count, span_len, nblocks, 128).transpose(2, 0, 1, 3)
    span_ids = jnp.arange(span_count).astype(jnp.int32)
    highest_precision = lax.Precision.HIGHEST

    def per_block(packed):
        in_part, grad_part, block_id = packed
        group_id = block_id * 128 // GSIZE
        nearby_dense_taps = jnp.concatenate([jnp.zeros((span_len,), jnp.float32), near_taps[group_id].astype(jnp.float32)])
        near_mat = toeplitz_matrix(nearby_dense_taps, span_len)
        conv_sum = jnp.einsum('ts,nsc->ntc', near_mat, in_part, precision=highest_precision)
        adjoint = jnp.einsum('ts,ntc->nsc', near_mat, grad_part, precision=highest_precision)
        near_corr = jnp.einsum('ntc,nsc->ts', grad_part, in_part, precision=highest_precision)
        near_grad = diagonal_totals(near_corr, span_len)[span_len:]
        far_list = []
        for slot_index in range(KB):
            lag_value = lag_blocks[group_id, slot_index]
            shifted = jnp.where((span_ids >= lag_value)[:, None, None], jnp.roll(in_part, lag_value, axis=0), 0.0)
            far_mat = toeplitz_matrix(distant_lag_taps[group_id, slot_index].astype(jnp.float32), span_len)
            conv_sum = conv_sum + jnp.einsum('ts,nsc->ntc', far_mat, shifted, precision=highest_precision)
            back_part = jnp.einsum('ts,ntc->nsc', far_mat, grad_part, precision=highest_precision)
            adjoint = adjoint + jnp.where((span_ids + lag_value < span_count)[:, None, None], jnp.roll(back_part, -lag_value, axis=0), 0.0)
            far_corr = jnp.einsum('ntc,nsc->ts', grad_part, shifted, precision=highest_precision)
            far_list.append(diagonal_totals(far_corr, span_len).at[0].set(0.0))
        return (conv_sum, adjoint, jnp.stack(far_list), near_grad)
    conv_all, adjoint_all, far_all, near_all = lax.map(per_block, (input_block_rows, grad_blocks, jnp.arange(nblocks).astype(jnp.int32)))
    conv_full = conv_all.transpose(1, 2, 0, 3).reshape(span_count * span_len, D)
    adjoint_full = adjoint_all.transpose(1, 2, 0, 3).reshape(span_count * span_len, D)
    block_out = (query_stream.astype(jnp.float32) * conv_full).astype(jnp.bfloat16)
    grad_values = (adjoint_full * key_stream.astype(jnp.float32)).astype(jnp.bfloat16)
    grad_scale = 1.0 / math.sqrt(span_count * span_len * GSIZE)
    grad_far = far_all.reshape(G, GSIZE // 128, KB, 2 * span_len).sum(axis=1) * grad_scale
    grad_near = near_all.reshape(G, GSIZE // 128, span_len).sum(axis=1) * grad_scale
    return (block_out, grad_values, grad_far, grad_near)
```

```python
import functools
import math

import jax
import jax.numpy as jnp
from jax import lax
from jax.experimental import pallas as pl
from jax.experimental.pallas import tpu as pltpu
from jax.sharding import PartitionSpec as P

GSIZE = 512
WIN = 4
VMEM_LIMIT = 48 * 1024 * 1024


def core_of():
    return lax.rem(lax.axis_index("ctx"), 2)


def block_group(meta, half, block, width, hw, bw):
    return lax.div(meta[1] * width + half * hw + block * bw, GSIZE)


def skew(taps, span):
    width = 2 * span
    row = pltpu.roll(jnp.broadcast_to(taps, (8, width)), span, 1)
    index = lax.broadcasted_iota(jnp.int32, (8, width), 0)
    for bit in (1, 2, 4):
        row = jnp.where((index & bit) != 0, pltpu.roll(row, bit, 1), row)
    filled = 8
    while filled < span:
        row = jnp.concatenate([row, pltpu.roll(row, filled, 1)], axis=0)
        filled *= 2
    return row[:, :span]


def diagonal_sums(matrix, span):
    width = 2 * span
    rows = jnp.concatenate([matrix, jnp.zeros((span, span), jnp.float32)], axis=1)
    half = span // 2
    while half >= 8:
        rows = rows[:half] + pltpu.roll(rows[half:], width - half, 1)
        half //= 2
    index = lax.broadcasted_iota(jnp.int32, (8, width), 0)
    for bit in (1, 2, 4):
        rows = jnp.where((index & bit) != 0, pltpu.roll(rows, width - bit, 1), rows)
    total = jnp.sum(rows, axis=0, keepdims=True)
    return pltpu.roll(jnp.broadcast_to(total, (8, width)), span, 1)[:1]


def params(*semantics):
    return pltpu.CompilerParams(
        dimension_semantics=semantics or None, vmem_limit_bytes=VMEM_LIMIT
    )


def stream_product(stream, frame, meta, key, value, query, grad):
    span, width = key.shape
    hw = width // 2
    cb = min(256, hw)
    steps = hw // cb
    mixed_core = 0 if stream == "P" else 1

    def index(is_mixed, i, meta):
        core = meta[0]
        half = core if frame == 0 else 1 - core
        wanted = (core == mixed_core) == is_mixed
        return (0, jnp.where(wanted, half * steps + i, 0))

    def body(meta, k_ref, v_ref, q_ref, g_ref, out_ref):
        f32 = jnp.float32

        @pl.when(meta[0] == mixed_core)
        def _():
            out_ref[...] = (k_ref[...].astype(f32) * v_ref[...].astype(f32)).astype(jnp.bfloat16)

        @pl.when(meta[0] != mixed_core)
        def _():
            out_ref[...] = (g_ref[...].astype(f32) * q_ref[...].astype(f32)).astype(jnp.bfloat16)

    mixed_spec = pl.BlockSpec((span, cb), functools.partial(index, True))
    gated_spec = pl.BlockSpec((span, cb), functools.partial(index, False))
    return pl.pallas_call(
        body,
        grid_spec=pltpu.PrefetchScalarGridSpec(
            num_scalar_prefetch=1,
            grid=(steps,),
            in_specs=[mixed_spec, mixed_spec, gated_spec, gated_spec],
            out_specs=pl.BlockSpec((span, cb), lambda i, meta: (0, i)),
        ),
        out_shape=jax.ShapeDtypeStruct((span, hw), jnp.bfloat16),
        compiler_params=params("arbitrary"),
        cost_estimate=pl.CostEstimate(flops=span * hw, bytes_accessed=6 * span * hw, transcendentals=0),
        name=f"own_{stream.lower()}{frame}",
    )(meta, key, value, query, grad)


def toeplitz_matrices(meta, tap_rows, span, width, hw, bw):
    nb = hw // bw
    slots1 = tap_rows.shape[2]

    def index(role, block, meta):
        core = meta[0]
        frame = lax.div(block, nb)
        half = jnp.where(frame == 0, core, 1 - core)
        group = block_group(meta, half, lax.rem(block, nb), width, hw, bw)
        return (jnp.where(core == 0, role, 1 - role), group, 0, 0)

    def body(meta, taps_ref, out_ref):
        for slot in range(slots1):
            taps = taps_ref[0, 0, pl.ds(slot, 1), :]
            out_ref[0, 0, slot] = skew(taps, span).astype(jnp.bfloat16)

    return pl.pallas_call(
        body,
        grid_spec=pltpu.PrefetchScalarGridSpec(
            num_scalar_prefetch=1,
            grid=(2, 2 * nb),
            in_specs=[pl.BlockSpec((1, 1, slots1, 2 * span), index)],
            out_specs=pl.BlockSpec(
                (1, 1, slots1, span, span), lambda role, block, meta: (role, block, 0, 0, 0)
            ),
        ),
        out_shape=jax.ShapeDtypeStruct((2, 2 * nb, slots1, span, span), jnp.bfloat16),
        compiler_params=params("arbitrary", "arbitrary"),
        cost_estimate=pl.CostEstimate(
            flops=20 * nb * slots1 * span * span, bytes_accessed=8 * nb * slots1 * span * span, transcendentals=0
        ),
        name="toeplitz",
    )(meta, tap_rows)


def pair(core, p_panel, q_panel):
    first = core == 0
    mixed = jnp.where(first, p_panel, q_panel)
    gated = jnp.where(first, q_panel, p_panel)
    return lax.dot_general(
        mixed, gated, (((1,), (1,)), ((), ())), preferred_element_type=jnp.float32
    )


def correlate_early(frame, meta, lags, p_own, q_own, x1, r1=None, x0=None):
    span, hw = p_own.shape
    bw = min(GSIZE, hw)
    nb = hw // bw
    slots = lags.shape[1]
    flat_lags = lags.reshape(-1)
    own = frame == 0
    width = 2 * hw

    def body(meta, lag_ref, *refs):
        if own:
            p_ref, q_ref, x1_ref, r1_ref, x0_ref, rows_ref, part_ref = refs
        else:
            p_ref, q_ref, x1_ref, rows_ref = refs
        core = meta[0]
        half = core if own else 1 - core
        group = block_group(meta, half, pl.program_id(0), width, hw, bw)
        rows_ref[0, pl.ds(0, 1), :] = diagonal_sums(pair(core, p_ref[...], q_ref[...]), span)
        for slot in range(slots):
            lag = lag_ref[group * slots + slot]
            place = pl.ds(1 + slot, 1)

            @pl.when(lag == 2)
            def _():
                rows_ref[0, place, :] = diagonal_sums(pair(core, p_ref[...], x1_ref[...]), span)

            if own:

                @pl.when(lag == 1)
                def _():
                    both = pair(core, r1_ref[...], q_ref[...]) + pair(core, p_ref[...], x0_ref[...])
                    rows_ref[0, place, :] = diagonal_sums(both, span)

            @pl.when((lag > 2) if own else (lag != 2))
            def _():
                rows_ref[0, place, :] = jnp.zeros((1, 2 * span), jnp.float32)

        if own:
            part_ref[0] = pair(core, r1_ref[...], x1_ref[...])

    panels = [p_own, q_own, x1] + ([r1, x0] if own else [])
    panel_spec = pl.BlockSpec((span, bw), lambda b, meta, lag: (0, b))
    out_specs = [pl.BlockSpec((1, slots + 1, 2 * span), lambda b, meta, lag: (b, 0, 0))]
    out_shape = [jax.ShapeDtypeStruct((nb, slots + 1, 2 * span), jnp.float32)]
    if own:
        out_specs.append(pl.BlockSpec((1, span, span), lambda b, meta, lag: (b, 0, 0)))
        out_shape.append(jax.ShapeDtypeStruct((nb, span, span), jnp.float32))
    return pl.pallas_call(
        body,
        grid_spec=pltpu.PrefetchScalarGridSpec(
            num_scalar_prefetch=2,
            grid=(nb,),
            in_specs=[panel_spec] * len(panels),
            out_specs=out_specs,
        ),
        out_shape=out_shape,
        compiler_params=params("arbitrary"),
        cost_estimate=pl.CostEstimate(
            flops=8 * span * span * hw, bytes_accessed=2 * len(panels) * span * hw, transcendentals=0
        ),
        name=f"correlate{frame}",
    )(meta, flat_lags, *panels)


def correlate_late(meta, lags, rows_own, rows_other, part, p_own, r2):
    span, hw = p_own.shape
    bw = min(GSIZE, hw)
    nb = hw // bw
    slots = lags.shape[1]
    width = 2 * hw

    def body(meta, lag_ref, own_ref, other_ref, part_ref, p_ref, r2_ref, out_ref):
        core = meta[0]
        for b in range(nb):
            columns = pl.ds(b * bw, bw)
            total = part_ref[b] + pair(core, p_ref[:, columns], r2_ref[:, columns])
            far = diagonal_sums(total, span)
            group = block_group(meta, core, b, width, hw, bw)
            rows = [own_ref[b, pl.ds(0, 1), :]]
            for slot in range(slots):
                lag = lag_ref[group * slots + slot]
                rows.append(jnp.where(lag == WIN - 1, far, own_ref[b, pl.ds(1 + slot, 1), :]))
            for slot in range(slots + 1):
                out_ref[core * nb + b, pl.ds(slot, 1), :] = rows[slot]
            out_ref[(1 - core) * nb + b] = other_ref[b]

    vmem = pl.BlockSpec(memory_space=pltpu.VMEM)
    smem = pl.BlockSpec(memory_space=pltpu.SMEM)
    return pl.pallas_call(
        body,
        in_specs=[smem, smem] + [vmem] * 5,
        out_specs=vmem,
        out_shape=jax.ShapeDtypeStruct((2 * nb, slots + 1, 2 * span), jnp.float32),
        compiler_params=params(),
        cost_estimate=pl.CostEstimate(
            flops=2 * span * span * hw, bytes_accessed=4 * span * hw, transcendentals=0
        ),
        name="correlate_last",
    )(meta, lags.reshape(-1), rows_own, rows_other, part, p_own, r2)


def gated_output(role, frame, meta, lags, toeplitz, own, lag1, lag2, lag3, key, query, results):
    span, hw = own.shape
    bw = min(GSIZE, hw)
    nb = hw // bw
    slots = lags.shape[1]
    width = 2 * hw
    role_at = 0 if role == "P" else 1
    block_core = 0 if role == "P" else 1

    def gate_index(is_query, b, meta, lag):
        core = meta[0]
        half = core if frame == 0 else 1 - core
        wanted = (core == block_core) == is_query
        return (0, jnp.where(wanted, half * nb + b, 0))

    def body(meta, lag_ref, t_ref, own_ref, a_ref, b_ref, c_ref, key_ref, query_ref, *rest):
        block_ref, values_ref, held, sems = rest[-4:]
        core = meta[0]
        half = core if frame == 0 else 1 - core
        step = pl.program_id(0)
        group = block_group(meta, half, step, width, hw, bw)
        total = jnp.dot(t_ref[0, 0, 0], own_ref[...], preferred_element_type=jnp.float32)
        for slot in range(slots):
            lag = lag_ref[group * slots + slot]
            panel = jnp.where(lag == 1, a_ref[...], jnp.where(lag == 2, b_ref[...], c_ref[...]))
            total = total + jnp.dot(t_ref[0, 0, 1 + slot], panel, preferred_element_type=jnp.float32)
        to_block = core == block_core
        gate = jnp.where(to_block, query_ref[...], key_ref[...]).astype(jnp.float32)
        held[step] = (total * gate).astype(jnp.bfloat16)

        def copy(at, out_ref):
            start = pl.multiple_of(half * hw + at * bw, 128)
            return pltpu.make_async_copy(held.at[at], out_ref.at[:, pl.ds(start, bw)], sems.at[at])

        for is_block, out_ref in ((True, block_ref), (False, values_ref)):

            @pl.when(to_block == is_block)
            def _():
                copy(step, out_ref).start()

                @pl.when(step == nb - 1)
                def _():
                    for at in range(nb):
                        copy(at, out_ref).wait()

    panel_spec = pl.BlockSpec((span, bw), lambda b, meta, lag: (0, b))
    in_specs = [
        pl.BlockSpec(
            (1, 1, slots + 1, span, span), lambda b, meta, lag: (role_at, frame * nb + b, 0, 0, 0)
        ),
        panel_spec,
        panel_spec,
        panel_spec,
        panel_spec,
        pl.BlockSpec((span, bw), functools.partial(gate_index, False)),
        pl.BlockSpec((span, bw), functools.partial(gate_index, True)),
    ]
    anywhere = pl.BlockSpec(memory_space=pl.ANY)
    aliases = {}
    if results:
        aliases = {2 + len(in_specs): 0, 3 + len(in_specs): 1}
        in_specs += [anywhere, anywhere]
    shape = jax.ShapeDtypeStruct((span, width), jnp.bfloat16)
    return pl.pallas_call(
        body,
        grid_spec=pltpu.PrefetchScalarGridSpec(
            num_scalar_prefetch=2,
            grid=(nb,),
            in_specs=in_specs,
            out_specs=[anywhere, anywhere],
            scratch_shapes=[
                pltpu.VMEM((nb, span, bw), jnp.bfloat16),
                pltpu.SemaphoreType.DMA((nb,)),
            ],
        ),
        out_shape=[shape, shape],
        input_output_aliases=aliases,
        compiler_params=params("arbitrary"),
        cost_estimate=pl.CostEstimate(
            flops=6 * span * span * hw, bytes_accessed=12 * span * hw, transcendentals=0
        ),
        name=f"out_{role.lower()}{frame}",
    )(meta, lags.reshape(-1), toeplitz, own, lag1, lag2, lag3, key, query, *results)


def after(value, *others):
    return lax.optimization_barrier((value,) + others)[0]


def sum_over_ctx(rows, core):
    count = lax.axis_size("ctx")
    chips = count // 2
    if count % 2 or chips > 4:
        return lax.psum(rows, "ctx")
    swap = [(i, i ^ 1) for i in range(count)]
    chip = lax.div(lax.axis_index("ctx"), 2)
    rows = rows + lax.ppermute(rows, "ctx", swap)
    arrived = []
    for hop in range(1, chips):
        moves = [(i, i + 2 * hop - 1 if i % 2 else i - 2 * hop + 1) for i in range(count)]
        moves = [(a, b) for a, b in moves if 0 <= b < count]
        arrived.append(lax.ppermute(rows, "ctx", moves))
    if not arrived:
        return rows
    mine = jnp.stack(arrived)
    theirs = lax.ppermute(mine, "ctx", swap)
    lower = jnp.where(core == 0, mine, theirs)
    upper = jnp.where(core == 0, theirs, mine)
    line = jnp.concatenate([lower[::-1], rows[None], upper], axis=0)
    in_order = lax.dynamic_slice_in_dim(line, chips - 1 - chip, chips, axis=0)
    return jnp.sum(in_order, axis=0)


def gather_over_chan(rows):
    count = lax.axis_size("chan")
    if count & (count - 1):
        return lax.all_gather(rows, "chan", axis=0, tiled=True)
    at = lax.axis_index("chan")
    bit = 1
    while bit < count:
        other = lax.ppermute(rows, "chan", [(i, i ^ bit) for i in range(count)])
        first = (at & bit) == 0
        rows = jnp.concatenate([jnp.where(first, rows, other), jnp.where(first, other, rows)], axis=0)
        bit *= 2
    return rows


def per_device(
    key_stream, value_stream, query_stream, grad_out, distant_lag_taps, near_taps, lag_blocks
):
    span, width = key_stream.shape
    groups, slots, doubled = distant_lag_taps.shape
    count = lax.axis_size("ctx")
    hw = width // 2
    bw = min(GSIZE, hw)
    core = core_of()
    meta = jnp.stack([core, lax.axis_index("chan")]).astype(jnp.int32)

    def keep(moves):
        return [(a, b) for a, b in moves if 0 <= b < count]

    swap = [(i, i ^ 1) for i in range(count)]
    to_near = keep([(i, i + 1 if i % 2 else i - 1) for i in range(count)])
    to_far = keep([(i, i - 3 if i % 2 else i + 3) for i in range(count)])
    onward = keep([(i, i - 2 if i % 2 else i + 2) for i in range(count)])

    def send(value, moves):
        return lax.ppermute(value, "ctx", moves)

    streams = (key_stream, value_stream, query_stream, grad_out)
    qa = stream_product("Q", 1, meta, *streams)
    r1a = send(qa, to_near)
    meta1 = after(meta, qa)
    qb = stream_product("Q", 0, meta1, *streams)
    r1b = send(qb, to_near)
    meta2 = after(meta1, qb)
    pa = stream_product("P", 1, meta2, *streams)
    pb = stream_product("P", 0, meta2, *streams)
    x0a, x0b = send(pa, swap), send(pb, swap)

    meta3, far_taps, near, lags = lax.optimization_barrier(
        (meta2, distant_lag_taps, near_taps, lag_blocks)
    )
    near_rows = jnp.concatenate([jnp.zeros_like(near), near], axis=1)[:, None, :]
    plain = jnp.concatenate([near_rows, far_taps], axis=1).astype(jnp.float32)
    flipped = jnp.roll(plain[:, :, ::-1], 1, axis=2)
    toeplitz = toeplitz_matrices(meta3, jnp.stack([flipped, plain]), span, width, hw, bw)

    r2a = send(after(pa, r1a), to_far)
    r2b = send(after(pb, r1a), to_far)
    r3a = send(after(r1a, r1b), onward)
    r3b = send(r1b, onward)
    x1a, x1b = send(r1a, swap), send(r1b, swap)

    rows_own, part = correlate_early(0, meta3, lags, pb, qb, x1b, r1a, x0a)
    (rows_other,) = correlate_early(1, meta3, lags, pa, qa, x1a)
    rows = correlate_late(meta3, lags, rows_own, rows_other, part, pb, r2a)

    x2a, x2b = send(r2a, swap), send(r2b, swap)
    gates = (key_stream, query_stream)
    results = gated_output("Q", 0, meta3, lags, toeplitz, qb, x0a, x1b, r2a, *gates, ())
    results = gated_output("Q", 1, meta3, lags, toeplitz, qa, x0b, x1a, r2b, *gates, results)
    results = gated_output("P", 0, meta3, lags, toeplitz, pb, r1a, x2b, r3a, *gates, results)
    results = gated_output("P", 1, meta3, lags, toeplitz, pa, r1b, x2a, r3b, *gates, results)

    rows = gather_over_chan(sum_over_ctx(rows, core))
    scale = 1.0 / math.sqrt(span * count * GSIZE)
    rows = rows.reshape(groups, GSIZE // bw, slots + 1, doubled).sum(axis=1) * scale
    return (results[0], results[1], rows[:, 1:], rows[:, 0, span:])


def solution(mesh):
    streams = P("ctx", "chan")
    return jax.shard_map(
        per_device,
        mesh=mesh,
        in_specs=(streams, streams, streams, streams, P(), P(), P()),
        out_specs=(streams, streams, P(), P()),
        check_vma=False,
    )
```

```python
import functools
import math

import jax
import jax.numpy as jnp
from jax import lax
from jax.experimental import pallas as pl
from jax.experimental.pallas import tpu as pltpu
from jax.sharding import PartitionSpec as P

GSIZE = 512
WIN = 4
VMEM_LIMIT = 16 * 1024 * 1024
FIRST_LIMIT = 60 * 1024 * 1024
SECOND_LIMIT = 16 * 1024 * 1024
SCALE = 32
BF16 = jnp.bfloat16
F32 = jnp.float32

VMEM = pl.BlockSpec(memory_space=pltpu.VMEM)
SMEM = pl.BlockSpec(memory_space=pltpu.SMEM)
HBM = pl.BlockSpec(memory_space=pltpu.HBM)


def core_of():
    return lax.rem(lax.axis_index("ctx"), 2)


def call(body, name, out_shape, in_specs, out_specs, scratch=(), aliases=None, limit=VMEM_LIMIT, flops=1):
    def run(*args):
        moved = sum(a.size * a.dtype.itemsize for a in args + tuple(jax.tree.leaves(out_shape)))
        return pl.pallas_call(
            body,
            in_specs=in_specs,
            out_specs=out_specs,
            out_shape=out_shape,
            scratch_shapes=scratch,
            input_output_aliases=aliases or {},
            compiler_params=pltpu.CompilerParams(vmem_limit_bytes=limit),
            cost_estimate=pl.CostEstimate(flops=flops, bytes_accessed=max(1, moved // SCALE), transcendentals=0),
            name=name,
        )(*args)

    return run


def block_group(half, block, width, bw):
    first = lax.axis_index("chan") * width + half * (width // 2) + block * bw
    return lax.div(first, GSIZE)


def rolled(value, shift):
    shift %= value.shape[1]
    if shift % 128 == 0:
        return value if shift == 0 else jnp.concatenate([value[:, -shift:], value[:, :-shift]], axis=1)
    return pltpu.roll(value, shift, 1)


def skew(taps, span):
    width = 2 * span
    row = rolled(jnp.broadcast_to(taps, (8, width)), span)
    index = lax.broadcasted_iota(jnp.int32, (8, width), 0)
    for bit in (1, 2, 4):
        row = jnp.where((index & bit) != 0, rolled(row, bit), row)
    filled = 8
    while filled < span:
        row = jnp.concatenate([row, rolled(row, filled)], axis=0)
        filled *= 2
    return row[:, :span]


def diagonal_sums(matrix, span):
    width = 2 * span
    rows = jnp.concatenate([matrix, jnp.zeros((span, span), F32)], axis=1)
    half = span // 2
    while half >= 8:
        rows = rows[:half] + rolled(rows[half:], -half)
        half //= 2
    index = lax.broadcasted_iota(jnp.int32, (8, width), 0)
    for bit in (1, 2, 4):
        rows = jnp.where((index & bit) != 0, rolled(rows, -bit), rows)
    return rolled(jnp.sum(rows, axis=0, keepdims=True), span)


def stream_products(wanted, streams, name, limit):
    span, width = streams[0].shape
    hw = width // 2
    kinds = sorted({kind[0] for kind in wanted}, reverse=True)

    def body(k_ref, v_ref, q_ref, g_ref, *rest):
        outs, (held, sems) = rest[:-2], rest[-2:]
        core = core_of()

        def copies(place, at, pair):
            half = 1 - core if at == 0 else core
            columns = pl.ds(pl.multiple_of(half * hw, 128), hw)
            return [
                pltpu.make_async_copy(ref.at[:, columns], held.at[place, at, i], sems.at[place, at, i])
                for i, ref in enumerate(pair)
            ]

        for place, kind in enumerate(kinds):
            mixed_core = 0 if kind == "P" else 1
            for is_mixed, pair in ((True, (k_ref, v_ref)), (False, (g_ref, q_ref))):

                @pl.when((core == mixed_core) == is_mixed)
                def _():
                    for at in range(2):
                        for copy in copies(place, at, pair):
                            copy.start()

        for place, kind in enumerate(kinds):
            for at in range(2):
                for copy in copies(place, at, (k_ref, v_ref)):
                    copy.wait()
                product = (held[place, at, 0].astype(F32) * held[place, at, 1].astype(F32)).astype(BF16)
                for out_ref, name in zip(outs, wanted):
                    if name == kind:
                        out_ref[at] = product
                    elif name == f"{kind}{at}":
                        out_ref[...] = product

    shapes = [jax.ShapeDtypeStruct((2, span, hw) if len(n) == 1 else (span, hw), BF16) for n in wanted]
    return call(
        body,
        name,
        shapes,
        [HBM] * 4,
        [VMEM] * len(shapes),
        [pltpu.VMEM((len(kinds), 2, 2, span, hw), BF16), pltpu.SemaphoreType.DMA((len(kinds), 2, 2))],
        limit=limit,
    )(*streams)


def short_lag(lag_ref, group, slots):
    lag = lag_ref[group * slots]
    for slot in range(1, slots):
        lag = jnp.minimum(lag, lag_ref[group * slots + slot])
    return lag


def toeplitz_matrices(lags, far_taps, near_taps, span, width, bw):
    groups, slots, doubled = far_taps.shape
    nb = width // 2 // bw

    def body(lag_ref, far_ref, near_ref, out_ref, near_rows):
        core = core_of()
        near_rows[...] = near_ref[...].astype(F32)
        for frame in range(2):
            half = core if frame == 0 else 1 - core
            for b in range(nb):
                group = block_group(half, b, width, bw)
                far = far_ref[group].astype(F32)
                near = near_rows[pl.ds(group, 1), :]
                short = last = jnp.zeros((1, doubled), F32)
                for slot in range(slots):
                    is_last = lag_ref[group * slots + slot] == WIN - 1
                    taps = far[slot : slot + 1]
                    short = jnp.where(is_last, short, taps)
                    last = jnp.where(is_last, taps, last)
                near = jnp.concatenate([jnp.zeros((1, span), F32), near], axis=1)
                for at, taps in enumerate((near, short, last)):
                    matrix = skew(taps, span)
                    out_ref[1 - core, frame * nb + b, at] = matrix.astype(BF16)
                    out_ref[core, frame * nb + b, at] = matrix.T.astype(BF16)

    return call(
        body,
        "toeplitz",
        jax.ShapeDtypeStruct((2, 2 * nb, 3, span, span), BF16),
        [SMEM, VMEM, VMEM],
        VMEM,
        [pltpu.VMEM((groups, span), F32)],
    )(lags, far_taps, near_taps)


def outer(mixed, gated):
    return lax.dot_general(mixed, gated, (((1,), (1,)), ((), ())), preferred_element_type=F32)


def by_core(body):
    core = core_of()

    @pl.when(core == 0)
    def _():
        body(outer)

    @pl.when(core != 0)
    def _():
        body(lambda p, q: outer(q, p))


def correlate_near(p_own, q_own):
    span, hw = p_own[0].shape
    bw = min(GSIZE, hw)
    nb = hw // bw

    def body(p0, p1, q0, q1, rows_ref):
        def run(pair):
            for frame in range(2):
                for b in range(nb):
                    at = pl.ds(b * bw, bw)
                    matrix = pair((p0, p1)[frame][:, at], (q0, q1)[frame][:, at])
                    rows_ref[frame, pl.ds(b, 1), :] = diagonal_sums(matrix, span)

        by_core(run)

    return call(
        body,
        "correlate_near",
        jax.ShapeDtypeStruct((2, nb, 2 * span), F32),
        [VMEM] * 4,
        VMEM,
    )(*p_own, *q_own)


def correlate_one(p_own, q_own, r1, x0):
    span, hw = p_own[0].shape
    bw = min(GSIZE, hw)
    nb = hw // bw

    def body(p_ref, q_ref, r1_ref, x0_ref, rows_ref):
        def run(pair):
            for b in range(nb):
                at = pl.ds(b * bw, bw)
                matrix = pair(r1_ref[0, :, at], q_ref[:, at]) + pair(p_ref[:, at], x0_ref[:, at])
                rows_ref[pl.ds(b, 1), :] = diagonal_sums(matrix, span)

        by_core(run)

    return call(
        body,
        "correlate_one",
        jax.ShapeDtypeStruct((nb, 2 * span), F32),
        [VMEM] * 4,
        VMEM,
    )(p_own[0], q_own[0], r1, x0[0])


def correlate_far(lags, slots, near, ones, p_own, r1, x1, r2):
    span, hw = r2.shape
    bw = min(GSIZE, hw)
    nb = hw // bw

    def body(lag_ref, near_ref, ones_ref, p0, p1, r1_ref, x1_ref, r2_ref, out_ref):
        core = core_of()

        def run(pair):
            for b in range(nb):
                at = pl.ds(b * bw, bw)
                p, x = p0[:, at], x1_ref[1, :, at]
                last = diagonal_sums(pair(r1_ref[0, :, at], x) + pair(p, r2_ref[:, at]), span)
                twos = [
                    diagonal_sums(pair(p, x), span),
                    diagonal_sums(pair(p1[:, at], x1_ref[0, :, at]), span),
                ]
                for frame in range(2):
                    half = core if frame == 0 else 1 - core
                    group = block_group(half, b, 2 * hw, bw)
                    place = half * nb + b
                    is_two = short_lag(lag_ref, group, slots) == 2
                    empty = jnp.zeros_like(last)
                    one = ones_ref[pl.ds(b, 1), :] if frame == 0 else empty
                    short = jnp.where(is_two, twos[frame], one)
                    distant = last if frame == 0 else empty
                    out_ref[place, pl.ds(0, 1), :] = near_ref[frame, pl.ds(b, 1), :]
                    for slot in range(slots):
                        is_last = lag_ref[group * slots + slot] == WIN - 1
                        out_ref[place, pl.ds(1 + slot, 1), :] = jnp.where(is_last, distant, short)

        by_core(run)

    return call(
        body,
        "correlate_far",
        jax.ShapeDtypeStruct((2 * nb, slots + 1, 2 * span), F32),
        [SMEM] + [VMEM] * 7,
        VMEM,
    )(lags, near, ones, *p_own, r1, x1, r2)


def partial_sums(lags, slots, toeplitz, p_own, r1, x2):
    span, hw = p_own[0].shape
    bw = min(GSIZE, hw)
    nb = hw // bw

    def body(lag_ref, t_ref, p0, p1, r1_ref, x20, x21, out_ref):
        core = core_of()
        for frame in range(2):
            half = core if frame == 0 else 1 - core
            for b in range(nb):
                at = pl.ds(b * bw, bw)
                group = block_group(half, b, 2 * hw, bw)
                is_one = short_lag(lag_ref, group, slots) == 1
                panel = jnp.where(is_one, r1_ref[frame, :, at], (x20, x21)[frame][:, at])
                total = jnp.dot(t_ref[0, frame * nb + b, 0], (p0, p1)[frame][:, at], preferred_element_type=F32)
                total += jnp.dot(t_ref[0, frame * nb + b, 1], panel, preferred_element_type=F32)
                out_ref[frame, :, at] = total

    return call(
        body,
        "partial_sums",
        jax.ShapeDtypeStruct((2, span, hw), F32),
        [SMEM] + [VMEM] * 6,
        VMEM,
    )(lags, toeplitz, *p_own, r1, *x2)


def gated_output(role, panels, total_of, key, query, results):
    span, width = key.shape
    hw = width // 2
    bw = min(GSIZE, hw)
    nb = hw // bw
    role_at = 0 if role == "P" else 1
    count = len(panels)

    def body(*refs):
        lag_ref, panel_refs, key_ref, query_ref = refs[0], refs[1:count], refs[count], refs[count + 1]
        block_ref, values_ref, gate, held, sems = refs[-5:]
        core = core_of()
        to_block = core == role_at

        def load(ref):
            return pltpu.make_async_copy(ref, gate, sems.at[2 * nb])

        def store(at, columns, ref):
            return pltpu.make_async_copy(held.at[at], ref.at[:, columns], sems.at[at])

        @pl.when(to_block)
        def _():
            load(query_ref).start()

        @pl.when(jnp.logical_not(to_block))
        def _():
            load(key_ref).start()

        for frame in range(2):
            half = core if frame == 0 else 1 - core
            for b in range(nb):
                at = frame * nb + b
                group = block_group(half, b, width, bw)
                total = total_of(lag_ref, group, frame, b, at, pl.ds(b * bw, bw), *panel_refs)
                if at == 0:
                    load(key_ref).wait()
                columns = pl.ds(pl.multiple_of(half * hw + b * bw, 128), bw)
                held[at] = (total * gate[:, columns].astype(F32)).astype(BF16)

                @pl.when(to_block)
                def _():
                    store(at, columns, block_ref).start()

                @pl.when(jnp.logical_not(to_block))
                def _():
                    store(at, columns, values_ref).start()

        for at in range(2 * nb):
            store(at, pl.ds(0, bw), block_ref).wait()

    shape = jax.ShapeDtypeStruct((span, width), BF16)
    return call(
        body,
        f"out_{role.lower()}",
        [shape, shape],
        [SMEM] + [VMEM] * (count - 1) + [HBM] * (2 + len(results)),
        [HBM, HBM],
        [
            pltpu.VMEM((span, width), BF16),
            pltpu.VMEM((2 * nb, span, bw), BF16),
            pltpu.SemaphoreType.DMA((2 * nb + 1,)),
        ],
        {count + 2: 0, count + 3: 1} if results else None,
    )(*panels, key, query, *results)


def q_output(lags, slots, toeplitz, q_own, x0, x1, r2, key, query):
    def total_of(lag_ref, group, frame, b, place, at, t_ref, q0, q1, x00, x01, x1_ref, r20, r21):
        is_one = short_lag(lag_ref, group, slots) == 1
        panel = jnp.where(is_one, (x00, x01)[frame][:, at], x1_ref[1 - frame, :, at])
        total = jnp.dot(t_ref[1, place, 0], (q0, q1)[frame][:, at], preferred_element_type=F32)
        total += jnp.dot(t_ref[1, place, 1], panel, preferred_element_type=F32)
        return total + jnp.dot(t_ref[1, place, 2], (r20, r21)[frame][:, at], preferred_element_type=F32)

    return gated_output("Q", (lags, toeplitz, *q_own, *x0, x1, *r2), total_of, key, query, ())


def p_output(lags, toeplitz, sums, r3, key, query, results):
    def total_of(lag_ref, group, frame, b, place, at, t_ref, sums_ref, r3_ref):
        last = jnp.dot(t_ref[0, place, 2], r3_ref[frame, :, at], preferred_element_type=F32)
        return sums_ref[frame, :, at] + last

    return gated_output("P", (lags, toeplitz, sums, r3), total_of, key, query, results)


def after(value, *others):
    return lax.optimization_barrier((value,) + others)[0]


def plain_sum(a, b):
    def body(a_ref, b_ref, out_ref):
        out_ref[...] = a_ref[...] + b_ref[...]

    return call(body, "add_rows", jax.ShapeDtypeStruct(a.shape, F32), [VMEM, VMEM], VMEM)(a, b)


def sum_over_chips(rows):
    count = lax.axis_size("ctx")
    if count & (count - 1):
        return lax.psum(rows, "ctx")
    bit = 2
    while bit < count:
        rows = plain_sum(rows, lax.ppermute(rows, "ctx", [(i, i ^ bit) for i in range(count)]))
        bit *= 2
    return rows


def sum_over_cores(rows):
    count = lax.axis_size("ctx")
    if count & (count - 1):
        return rows
    return plain_sum(rows, lax.ppermute(rows, "ctx", [(i, i ^ 1) for i in range(count)]))


def joined(first, second, bit):
    def body(first_ref, second_ref, out_ref):
        length = first_ref.shape[0]
        here = lax.rem(lax.div(lax.axis_index("chan"), bit), 2)
        out_ref[pl.ds(here * length, length)] = first_ref[...]
        out_ref[pl.ds((1 - here) * length, length)] = second_ref[...]

    shape = jax.ShapeDtypeStruct((2 * first.shape[0],) + first.shape[1:], F32)
    return call(body, "join_rows", shape, [VMEM] * 2, VMEM)(first, second)


def filter_gradients(rows, groups, span, scale):
    count = lax.axis_size("chan")
    _, rows_per, doubled = rows.shape
    slots = rows_per - 1
    if count & (count - 1):
        rows = lax.all_gather(rows, "chan", axis=0, tiled=True)
    else:
        bit = 1
        while bit < count:
            other = lax.ppermute(rows, "chan", [(i, i ^ bit) for i in range(count)])
            rows = joined(rows, other, bit)
            bit *= 2
    repeat = rows.shape[0] // groups

    def body(rows_ref, far_ref, near_ref):
        for group in range(groups):
            total = rows_ref[group * repeat]
            for at in range(1, repeat):
                total = total + rows_ref[group * repeat + at]
            far_ref[group] = total[1:] * scale
            near_ref[pl.ds(group, 1), :] = total[:1, span:] * scale

    return call(
        body,
        "filter_gradients",
        [
            jax.ShapeDtypeStruct((groups, slots, doubled), F32),
            jax.ShapeDtypeStruct((groups, span), F32),
        ],
        [VMEM],
        [VMEM, VMEM],
    )(rows)


def per_device(
    key_stream, value_stream, query_stream, grad_out, distant_lag_taps, near_taps, lag_blocks
):
    span, width = key_stream.shape
    groups = distant_lag_taps.shape[0]
    count = lax.axis_size("ctx")
    hw = width // 2
    bw = min(GSIZE, hw)

    def keep(moves):
        return [(a, b) for a, b in moves if 0 <= b < count]

    swap = [(i, i ^ 1) for i in range(count)]
    to_near = keep([(i, i + 1 if i % 2 else i - 1) for i in range(count)])
    to_far = keep([(i, i - 3 if i % 2 else i + 3) for i in range(count)])
    onward = keep([(i, i - 2 if i % 2 else i + 2) for i in range(count)])

    def send(value, moves):
        return lax.ppermute(value, "ctx", moves)

    slots = lag_blocks.shape[1]
    streams = (key_stream, value_stream, query_stream, grad_out)
    (q_sent,) = stream_products(("Q",), streams, "q_stream", FIRST_LIMIT)
    r1 = send(q_sent, to_near)
    *late, far_taps, near_taps, lags, _ = lax.optimization_barrier(
        streams + (distant_lag_taps, near_taps, lag_blocks, q_sent)
    )
    lags = lags.reshape(-1)
    qa, qb, pa, pb = stream_products(("Q0", "Q1", "P0", "P1"), late, "streams", SECOND_LIMIT)
    q_own, p_own = (qb, qa), (pb, pa)
    x0 = (send(pa, swap), send(pb, swap))
    toeplitz = toeplitz_matrices(lags, far_taps, near_taps, span, width, bw)
    near = correlate_near(p_own, q_own)

    r1, x0 = lax.optimization_barrier((r1, x0, toeplitz, near))[:2]
    r2a = send(after(pa, r1), to_far)
    x1 = send(r1, swap)
    ones = correlate_one(p_own, q_own, r1, x0)
    r2b = send(after(pb, x1), to_far)
    rows = sum_over_chips(correlate_far(lags, slots, near, ones, p_own, r1, x1, r2a))
    r1_late, r2a_late, r2b, rows = lax.optimization_barrier((r1, r2a, r2b, rows))
    r3 = send(r1_late, onward)
    x2 = (send(r2b, swap), send(r2a_late, swap))
    results = q_output(lags, slots, toeplitz, q_own, x0, x1, (r2a, r2b), key_stream, query_stream)
    rows = sum_over_cores(rows)
    sums = partial_sums(lags, slots, toeplitz, p_own, r1, x2)
    results = p_output(lags, toeplitz, sums, r3, key_stream, query_stream, results)

    scale = 1.0 / math.sqrt(span * count * GSIZE)
    far, near = filter_gradients(rows, groups, span, scale)
    return (results[0], results[1], far, near)


def solution(mesh):
    streams = P("ctx", "chan")
    return jax.shard_map(
        per_device,
        mesh=mesh,
        in_specs=(streams, streams, streams, streams, P(), P(), P()),
        out_specs=(streams, streams, P(), P()),
        check_vma=False,
    )
```

```python
import functools
import math

import jax
import jax.numpy as jnp
from jax import lax
from jax.experimental import pallas as pl
from jax.experimental.pallas import tpu as pltpu
from jax.sharding import PartitionSpec as P

GSIZE = 512
WIN = 4
VMEM_LIMIT = 16 * 1024 * 1024
SCALE = 1
BF16 = jnp.bfloat16
F32 = jnp.float32

VMEM = pl.BlockSpec(memory_space=pltpu.VMEM)
SMEM = pl.BlockSpec(memory_space=pltpu.SMEM)
HBM = pl.BlockSpec(memory_space=pltpu.HBM)


def core_of():
    return lax.rem(lax.axis_index("ctx"), 2)


def call(body, name, out_shape, in_specs, out_specs, scratch=(), aliases=None, limit=VMEM_LIMIT, flops=1):
    def run(*args):
        moved = sum(a.size * a.dtype.itemsize for a in args + tuple(jax.tree.leaves(out_shape)))
        return pl.pallas_call(
            body,
            in_specs=in_specs,
            out_specs=out_specs,
            out_shape=out_shape,
            scratch_shapes=scratch,
            input_output_aliases=aliases or {},
            compiler_params=pltpu.CompilerParams(vmem_limit_bytes=limit),
            cost_estimate=pl.CostEstimate(flops=flops, bytes_accessed=max(1, moved // SCALE), transcendentals=0),
            name=name,
        )(*args)

    return run


def block_group(half, block, width, bw):
    first = lax.axis_index("chan") * width + half * (width // 2) + block * bw
    return lax.div(first, GSIZE)


def rolled(value, shift):
    shift %= value.shape[1]
    if shift % 128 == 0:
        return value if shift == 0 else jnp.concatenate([value[:, -shift:], value[:, :-shift]], axis=1)
    return pltpu.roll(value, shift, 1)


def skew(taps, span):
    width = 2 * span
    row = rolled(jnp.broadcast_to(taps, (8, width)), span)
    index = lax.broadcasted_iota(jnp.int32, (8, width), 0)
    for bit in (1, 2, 4):
        row = jnp.where((index & bit) != 0, rolled(row, bit), row)
    filled = 8
    while filled < span:
        row = jnp.concatenate([row, rolled(row, filled)], axis=0)
        filled *= 2
    return row[:, :span]


def diagonal_sums(matrix, span):
    width = 2 * span
    rows = jnp.concatenate([matrix, jnp.zeros((span, span), F32)], axis=1)
    half = span // 2
    while half >= 8:
        rows = rows[:half] + rolled(rows[half:], -half)
        half //= 2
    index = lax.broadcasted_iota(jnp.int32, (8, width), 0)
    for bit in (1, 2, 4):
        rows = jnp.where((index & bit) != 0, rolled(rows, -bit), rows)
    return rolled(jnp.sum(rows, axis=0, keepdims=True), span)


def stream_products(wanted, streams, name):
    span, width = streams[0].shape
    hw = width // 2
    count = len(wanted)

    def body(k_ref, v_ref, q_ref, g_ref, *rest):
        outs, (held, sems) = rest[:-2], rest[-2:]
        core = core_of()

        def copies(at, pair):
            half = 1 - core if wanted[at][1] == "0" else core
            columns = pl.ds(pl.multiple_of(half * hw, 128), hw)
            return [
                pltpu.make_async_copy(ref.at[:, columns], held.at[at, i], sems.at[at, i])
                for i, ref in enumerate(pair)
            ]

        for at, kind in enumerate(wanted):
            mixed_core = 0 if kind[0] == "P" else 1
            for is_mixed, pair in ((True, (k_ref, v_ref)), (False, (g_ref, q_ref))):

                @pl.when((core == mixed_core) == is_mixed)
                def _():
                    for copy in copies(at, pair):
                        copy.start()

        for at in range(count):
            for copy in copies(at, (k_ref, v_ref)):
                copy.wait()
            product = (held[at, 0].astype(F32) * held[at, 1].astype(F32)).astype(BF16)
            outs[at][...] = product

    return call(
        body,
        name,
        [jax.ShapeDtypeStruct((span, hw), BF16)] * count,
        [HBM] * 4,
        [VMEM] * count,
        [pltpu.VMEM((count, 2, span, hw), BF16), pltpu.SemaphoreType.DMA((count, 2))],
    )(*streams)


def short_lag(lag_ref, group, slots):
    lag = lag_ref[group * slots]
    for slot in range(1, slots):
        lag = jnp.minimum(lag, lag_ref[group * slots + slot])
    return lag


def toeplitz_matrices(lags, far_taps, near_taps, span, width, bw):
    groups, slots, doubled = far_taps.shape
    nb = width // 2 // bw

    def body(lag_ref, far_ref, near_ref, out_ref, near_rows):
        core = core_of()
        near_rows[...] = near_ref[...].astype(F32)
        for frame in range(2):
            half = core if frame == 0 else 1 - core
            for b in range(nb):
                group = block_group(half, b, width, bw)
                far = far_ref[group].astype(F32)
                near = near_rows[pl.ds(group, 1), :]
                short = last = jnp.zeros((1, doubled), F32)
                for slot in range(slots):
                    is_last = lag_ref[group * slots + slot] == WIN - 1
                    taps = far[slot : slot + 1]
                    short = jnp.where(is_last, short, taps)
                    last = jnp.where(is_last, taps, last)
                near = jnp.concatenate([jnp.zeros((1, span), F32), near], axis=1)
                for at, taps in enumerate((near, short, last)):
                    matrix = skew(taps, span)
                    out_ref[1 - core, frame * nb + b, at] = matrix.astype(BF16)
                    out_ref[core, frame * nb + b, at] = matrix.T.astype(BF16)

    return call(
        body,
        "toeplitz",
        jax.ShapeDtypeStruct((2, 2 * nb, 3, span, span), BF16),
        [SMEM, VMEM, VMEM],
        VMEM,
        [pltpu.VMEM((groups, span), F32)],
    )(lags, far_taps, near_taps)


def outer(mixed, gated):
    return lax.dot_general(mixed, gated, (((1,), (1,)), ((), ())), preferred_element_type=F32)


def by_core(body):
    core = core_of()

    @pl.when(core == 0)
    def _():
        body(outer)

    @pl.when(core != 0)
    def _():
        body(lambda p, q: outer(q, p))


def correlate_near(p_own, q_own):
    span, hw = p_own[0].shape
    bw = min(GSIZE, hw)
    nb = hw // bw

    def body(p0, p1, q0, q1, rows_ref):
        def run(pair):
            for frame in range(2):
                for b in range(nb):
                    at = pl.ds(b * bw, bw)
                    matrix = pair((p0, p1)[frame][:, at], (q0, q1)[frame][:, at])
                    rows_ref[frame, pl.ds(b, 1), :] = diagonal_sums(matrix, span)

        by_core(run)

    return call(
        body,
        "correlate_near",
        jax.ShapeDtypeStruct((2, nb, 2 * span), F32),
        [VMEM] * 4,
        VMEM,
    )(*p_own, *q_own)


def correlate_far(lags, slots, near, p_own, q_own, r1, x0, x1, r2):
    span, hw = r2.shape
    bw = min(GSIZE, hw)
    nb = hw // bw

    def body(lag_ref, near_ref, p0, p1, q_ref, r1_ref, x0_ref, x10, x11, r2_ref, out_ref):
        core = core_of()

        def run(pair):
            for b in range(nb):
                at = pl.ds(b * bw, bw)
                p, x, r = p0[:, at], x10[:, at], r1_ref[:, at]
                is_one = short_lag(lag_ref, block_group(core, b, 2 * hw, bw), slots) == 1
                short = pair(jnp.where(is_one, r, p), jnp.where(is_one, q_ref[:, at], x))
                short += pair(p, jnp.where(is_one, x0_ref[:, at], jnp.zeros_like(p)))
                last = pair(r, x) + pair(p, r2_ref[:, at])
                other = pair(p1[:, at], x11[:, at])
                rows = [diagonal_sums(matrix, span) for matrix in (short, last, other)]
                empty = jnp.zeros_like(rows[0])
                for frame in range(2):
                    half = core if frame == 0 else 1 - core
                    group = block_group(half, b, 2 * hw, bw)
                    place = half * nb + b
                    if frame == 0:
                        close, distant = rows[0], rows[1]
                    else:
                        close = jnp.where(short_lag(lag_ref, group, slots) == 2, rows[2], empty)
                        distant = empty
                    out_ref[place, pl.ds(0, 1), :] = near_ref[frame, pl.ds(b, 1), :]
                    for slot in range(slots):
                        is_last = lag_ref[group * slots + slot] == WIN - 1
                        out_ref[place, pl.ds(1 + slot, 1), :] = jnp.where(is_last, distant, close)

        by_core(run)

    return call(
        body,
        "correlate_far",
        jax.ShapeDtypeStruct((2 * nb, slots + 1, 2 * span), F32),
        [SMEM] + [VMEM] * 9,
        VMEM,
    )(lags, near, *p_own, q_own[0], r1, x0, *x1, r2)


def partial_sums(lags, slots, toeplitz, p_own, r1, x2, key, query):
    span, hw = p_own[0].shape
    bw = min(GSIZE, hw)
    nb = hw // bw

    def body(lag_ref, t_ref, p0, p1, r10, r11, x20, x21, key_ref, query_ref, gate_ref, out_ref, sem):
        core = core_of()

        def load(ref):
            return pltpu.make_async_copy(ref, gate_ref, sem)

        @pl.when(core == 0)
        def _():
            load(query_ref).start()

        @pl.when(core != 0)
        def _():
            load(key_ref).start()

        for frame in range(2):
            half = core if frame == 0 else 1 - core
            for b in range(nb):
                at = pl.ds(b * bw, bw)
                group = block_group(half, b, 2 * hw, bw)
                is_one = short_lag(lag_ref, group, slots) == 1
                panel = jnp.where(is_one, (r10, r11)[frame][:, at], (x20, x21)[frame][:, at])
                total = jnp.dot(t_ref[0, frame * nb + b, 0], (p0, p1)[frame][:, at], preferred_element_type=F32)
                total += jnp.dot(t_ref[0, frame * nb + b, 1], panel, preferred_element_type=F32)
                out_ref[frame, :, at] = total
        load(key_ref).wait()

    return call(
        body,
        "partial_sums",
        [jax.ShapeDtypeStruct((span, 2 * hw), BF16), jax.ShapeDtypeStruct((2, span, hw), F32)],
        [SMEM] + [VMEM] * 7 + [HBM] * 2,
        [VMEM, VMEM],
        [pltpu.SemaphoreType.DMA],
    )(lags, toeplitz, *p_own, *r1, *x2, key, query)


def gated_output(role, panels, total_of, gates, results):
    span, width = gates[0].shape
    hw = width // 2
    bw = min(GSIZE, hw)
    nb = hw // bw
    role_at = 0 if role == "P" else 1
    count = len(panels)
    loads = len(gates) == 2

    def body(*refs):
        lag_ref, panel_refs, gate_refs = refs[0], refs[1:count], refs[count : count + len(gates)]
        block_ref, values_ref, held, sems = refs[-4 - loads : len(refs) - loads]
        core = core_of()
        to_block = core == role_at
        gate = refs[-1] if loads else gate_refs[0]

        def load(ref):
            return pltpu.make_async_copy(ref, gate, sems.at[2 * nb])

        def store(at, columns, ref):
            return pltpu.make_async_copy(held.at[at], ref.at[:, columns], sems.at[at])

        if loads:

            @pl.when(to_block)
            def _():
                load(gate_refs[1]).start()

            @pl.when(jnp.logical_not(to_block))
            def _():
                load(gate_refs[0]).start()

        for frame in range(2):
            half = core if frame == 0 else 1 - core
            for b in range(nb):
                at = frame * nb + b
                group = block_group(half, b, width, bw)
                total = total_of(lag_ref, group, frame, b, at, pl.ds(b * bw, bw), *panel_refs)
                if at == 0 and loads:
                    load(gate_refs[0]).wait()
                columns = pl.ds(pl.multiple_of(half * hw + b * bw, 128), bw)
                held[at] = (total * gate[:, columns].astype(F32)).astype(BF16)

                @pl.when(to_block)
                def _():
                    store(at, columns, block_ref).start()

                @pl.when(jnp.logical_not(to_block))
                def _():
                    store(at, columns, values_ref).start()

        for at in range(2 * nb):
            store(at, pl.ds(0, bw), block_ref).wait()

    shape = jax.ShapeDtypeStruct((span, width), BF16)
    scratch = [pltpu.VMEM((2 * nb, span, bw), BF16), pltpu.SemaphoreType.DMA((2 * nb + 1,))]
    if loads:
        scratch.append(pltpu.VMEM((span, width), BF16))
    first = count + len(gates)
    return call(
        body,
        f"out_{role.lower()}",
        [shape, shape],
        [SMEM] + [VMEM] * (count - 1) + [HBM if loads else VMEM] * len(gates) + [HBM] * len(results),
        [HBM, HBM],
        scratch,
        {first: 0, first + 1: 1} if results else None,
    )(*panels, *gates, *results)


def q_output(lags, slots, toeplitz, q_own, x0, x1, r2, key, query):
    def total_of(lag_ref, group, frame, b, place, at, t_ref, q0, q1, x00, x01, x10, x11, r20, r21):
        is_one = short_lag(lag_ref, group, slots) == 1
        panel = jnp.where(is_one, (x00, x01)[frame][:, at], (x10, x11)[frame][:, at])
        total = jnp.dot(t_ref[1, place, 0], (q0, q1)[frame][:, at], preferred_element_type=F32)
        total += jnp.dot(t_ref[1, place, 1], panel, preferred_element_type=F32)
        return total + jnp.dot(t_ref[1, place, 2], (r20, r21)[frame][:, at], preferred_element_type=F32)

    return gated_output("Q", (lags, toeplitz, *q_own, *x0, *x1, *r2), total_of, (key, query), ())


def p_output(lags, toeplitz, sums, r3, gate, results):
    def total_of(lag_ref, group, frame, b, place, at, t_ref, sums_ref, r3_ref):
        last = jnp.dot(t_ref[0, place, 2], r3_ref[frame, :, at], preferred_element_type=F32)
        return sums_ref[frame, :, at] + last

    return gated_output("P", (lags, toeplitz, sums, r3), total_of, (gate,), results)


def after(value, *others):
    return lax.optimization_barrier((value,) + others)[0]


def stacked(parts):
    def body(*refs):
        for i, ref in enumerate(refs[:-1]):
            refs[-1][i] = ref[...]

    shape = jax.ShapeDtypeStruct((len(parts),) + parts[0].shape, parts[0].dtype)
    return call(body, "stack", shape, [VMEM] * len(parts), VMEM)(*parts)


def added(parts):
    def body(*refs):
        terms = [ref[...] for ref in refs[:-1]]
        while len(terms) > 1:
            terms = [a + b for a, b in zip(terms[::2], terms[1::2])]
        refs[-1][...] = terms[0]

    shape = jax.ShapeDtypeStruct(parts[0].shape, F32)
    return call(body, "add_rows", shape, [VMEM] * len(parts), VMEM)(*parts)


def sum_over_chips(rows, work):
    count = lax.axis_size("ctx")
    if count & (count - 1):
        return lax.psum(rows, "ctx")
    bit = 2
    while bit < count:
        steps = [k * bit for k in range(1, 4) if k * bit < count]
        others = [lax.ppermute(rows, "ctx", [(i, i ^ step) for i in range(count)]) for step in steps]
        if bit == 2:
            others = lax.optimization_barrier((others, work))[0]
        rows = added([rows] + others)
        bit *= 4
    return rows


def sum_over_cores(rows):
    count = lax.axis_size("ctx")
    if count & (count - 1):
        return rows
    return added([rows, lax.ppermute(rows, "ctx", [(i, i ^ 1) for i in range(count)])])


def joined(first, second, bit):
    def body(first_ref, second_ref, out_ref):
        length = first_ref.shape[0]
        here = lax.rem(lax.div(lax.axis_index("chan"), bit), 2)
        out_ref[pl.ds(here * length, length)] = first_ref[...]
        out_ref[pl.ds((1 - here) * length, length)] = second_ref[...]

    shape = jax.ShapeDtypeStruct((2 * first.shape[0],) + first.shape[1:], F32)
    return call(body, "join_rows", shape, [VMEM] * 2, VMEM)(first, second)


def gather_over_chan(rows, work):
    count = lax.axis_size("chan")
    if count & (count - 1):
        return lax.all_gather(rows, "chan", axis=0, tiled=True)
    bit = 1
    while bit < count:
        other = lax.ppermute(rows, "chan", [(i, i ^ bit) for i in range(count)])
        if bit == 1:
            other = after(other, work)
        rows = joined(rows, other, bit)
        bit *= 2
    return rows


def filter_gradients(rows, groups, span, scale):
    _, rows_per, doubled = rows.shape
    slots = rows_per - 1
    repeat = rows.shape[0] // groups

    def body(rows_ref, far_ref, near_ref):
        for group in range(groups):
            total = rows_ref[group * repeat]
            for at in range(1, repeat):
                total = total + rows_ref[group * repeat + at]
            far_ref[group] = total[1:] * scale
            near_ref[pl.ds(group, 1), :] = total[:1, span:] * scale

    return call(
        body,
        "filter_gradients",
        [
            jax.ShapeDtypeStruct((groups, slots, doubled), F32),
            jax.ShapeDtypeStruct((groups, span), F32),
        ],
        [VMEM],
        [VMEM, VMEM],
    )(rows)


def per_device(
    key_stream, value_stream, query_stream, grad_out, distant_lag_taps, near_taps, lag_blocks
):
    span, width = key_stream.shape
    groups = distant_lag_taps.shape[0]
    count = lax.axis_size("ctx")
    hw = width // 2
    bw = min(GSIZE, hw)

    def keep(moves):
        return [(a, b) for a, b in moves if 0 <= b < count]

    swap = [(i, i ^ 1) for i in range(count)]
    to_near = keep([(i, i + 1 if i % 2 else i - 1) for i in range(count)])
    to_far = keep([(i, i - 3 if i % 2 else i + 3) for i in range(count)])
    onward = keep([(i, i - 2 if i % 2 else i + 2) for i in range(count)])

    def send(value, moves):
        return lax.ppermute(value, "ctx", moves)

    slots = lag_blocks.shape[1]
    streams = (key_stream, value_stream, query_stream, grad_out)
    streams = tuple(pltpu.with_memory_space_constraint(x, pltpu.HBM) for x in streams)
    qa, qb = stream_products(("Q0", "Q1"), streams, "q_stream")
    r1a, r1b = send(qa, to_near), send(qb, to_near)
    *late, far_taps, near_taps, lags, _ = lax.optimization_barrier(
        streams + (distant_lag_taps, near_taps, lag_blocks, qb)
    )
    lags = lags.reshape(-1)
    pa, pb = stream_products(("P0", "P1"), late, "p_stream")
    q_own, p_own = (qb, qa), (pb, pa)
    toeplitz = toeplitz_matrices(lags, far_taps, near_taps, span, width, bw)
    near = correlate_near(p_own, q_own)

    r2a = send(after(pa, near, toeplitz), to_far)
    r1 = lax.optimization_barrier(((r1a, r1b), toeplitz, near))[0]
    x1 = (send(r1[1], swap), send(r1[0], swap))
    x0a = send(after(pa, r1), swap)
    r2b = send(after(pb, r1), to_far)
    both, r1 = lax.optimization_barrier((stacked(r1), r1))
    rows = correlate_far(lags, slots, near, p_own, q_own, r1[0], x0a, x1, r2a)
    x0b = send(after(pb, rows), swap)

    gates = (key_stream, query_stream)
    results = q_output(lags, slots, toeplitz, q_own, (x0a, x0b), x1, (r2a, r2b), *gates)
    rows = sum_over_chips(rows, results[0])
    both, r2_late, rows = lax.optimization_barrier((both, (r2a, r2b), rows))
    r3 = send(both, onward)
    x2 = (send(r2_late[1], swap), send(r2_late[0], swap))
    rows = sum_over_cores(rows)
    gate, sums = partial_sums(lags, slots, toeplitz, p_own, r1, x2, *gates)
    rows = gather_over_chan(rows, sums)
    scale = 1.0 / math.sqrt(span * count * GSIZE)
    far, near = filter_gradients(rows, groups, span, scale)
    results = p_output(lags, toeplitz, sums, r3, gate, results)
    return (results[0], results[1], far, near)


def solution(mesh):
    streams = P("ctx", "chan")
    return jax.shard_map(
        per_device,
        mesh=mesh,
        in_specs=(streams, streams, streams, streams, P(), P(), P()),
        out_specs=(streams, streams, P(), P()),
        check_vma=False,
    )
```

```python
import functools
import math

import jax
import jax.numpy as jnp
from jax import lax
from jax.experimental import pallas as pl
from jax.experimental.pallas import tpu as pltpu
from jax.sharding import PartitionSpec as P

GSIZE = 512
WIN = 4

Q_OUTPUT_FLOPS = 46 * 10**8
VMEM_LIMIT = 16 * 1024 * 1024
SCALE = 1
BF16 = jnp.bfloat16
F32 = jnp.float32

VMEM = pl.BlockSpec(memory_space=pltpu.VMEM)
SMEM = pl.BlockSpec(memory_space=pltpu.SMEM)
HBM = pl.BlockSpec(memory_space=pltpu.HBM)


def core_of():
    return lax.rem(lax.axis_index("ctx"), 2)


def call(body, name, out_shape, in_specs, out_specs, scratch=(), aliases=None, limit=VMEM_LIMIT, flops=1):
    def run(*args):
        moved = sum(a.size * a.dtype.itemsize for a in args + tuple(jax.tree.leaves(out_shape)))
        return pl.pallas_call(
            body,
            in_specs=in_specs,
            out_specs=out_specs,
            out_shape=out_shape,
            scratch_shapes=scratch,
            input_output_aliases=aliases or {},
            compiler_params=pltpu.CompilerParams(vmem_limit_bytes=limit),
            cost_estimate=pl.CostEstimate(flops=flops, bytes_accessed=max(1, moved // SCALE), transcendentals=0),
            name=name,
        )(*args)

    return run


def valid(stream, lag):
    place = lax.axis_index("ctx")
    earlier, later = place >= lag, place + lag < lax.axis_size("ctx")
    return jnp.where(core_of() == (0 if stream == "P" else 1), earlier, later)


def kept(panel, exists):
    return jnp.where(exists, panel, jnp.zeros_like(panel))


def block_group(half, block, width, bw):
    first = lax.axis_index("chan") * width + half * (width // 2) + block * bw
    return lax.div(first, GSIZE)


def rolled(value, shift):
    shift %= value.shape[1]
    if shift % 128 == 0:
        return value if shift == 0 else jnp.concatenate([value[:, -shift:], value[:, :-shift]], axis=1)
    return pltpu.roll(value, shift, 1)


def skew(taps, span):
    width = 2 * span
    row = rolled(jnp.broadcast_to(taps, (8, width)), span)
    index = lax.broadcasted_iota(jnp.int32, (8, width), 0)
    for bit in (1, 2, 4):
        row = jnp.where((index & bit) != 0, rolled(row, bit), row)
    filled = 8
    while filled < span:
        row = jnp.concatenate([row, rolled(row, filled)], axis=0)
        filled *= 2
    return row[:, :span]


def diagonal_sums(matrix, span):
    width = 2 * span
    rows = jnp.concatenate([matrix, jnp.zeros((span, span), F32)], axis=1)
    half = span // 2
    while half >= 8:
        rows = rows[:half] + rolled(rows[half:], -half)
        half //= 2
    index = lax.broadcasted_iota(jnp.int32, (8, width), 0)
    for bit in (1, 2, 4):
        rows = jnp.where((index & bit) != 0, rolled(rows, -bit), rows)
    return rolled(jnp.sum(rows, axis=0, keepdims=True), span)


def stream_products(wanted, streams, name):
    span, width = streams[0].shape
    hw = width // 2
    count = len(wanted)

    def body(k_ref, v_ref, q_ref, g_ref, *rest):
        outs, (held, sems) = rest[:-2], rest[-2:]
        core = core_of()

        def copies(at, pair):
            half = 1 - core if wanted[at][1] == "0" else core
            columns = pl.ds(pl.multiple_of(half * hw, 128), hw)
            return [
                pltpu.make_async_copy(ref.at[:, columns], held.at[at, i], sems.at[at, i])
                for i, ref in enumerate(pair)
            ]

        for at, kind in enumerate(wanted):
            mixed_core = 0 if kind[0] == "P" else 1
            for is_mixed, pair in ((True, (k_ref, v_ref)), (False, (g_ref, q_ref))):

                @pl.when((core == mixed_core) == is_mixed)
                def _():
                    for copy in copies(at, pair):
                        copy.start()

        for at in range(count):
            for copy in copies(at, (k_ref, v_ref)):
                copy.wait()
            product = (held[at, 0].astype(F32) * held[at, 1].astype(F32)).astype(BF16)
            outs[at][...] = product

    return call(
        body,
        name,
        [jax.ShapeDtypeStruct((span, hw), BF16)] * count,
        [HBM] * 4,
        [VMEM] * count,
        [pltpu.VMEM((count, 2, span, hw), BF16), pltpu.SemaphoreType.DMA((count, 2))],
    )(*streams)


def short_lag(lag_ref, group, slots):
    lag = lag_ref[group * slots]
    for slot in range(1, slots):
        lag = jnp.minimum(lag, lag_ref[group * slots + slot])
    return lag


def toeplitz_matrices(lags, far_taps, near_taps, span, width, bw):
    groups, slots, doubled = far_taps.shape
    nb = width // 2 // bw

    def body(lag_ref, far_ref, near_ref, out_ref, near_rows):
        core = core_of()
        near_rows[...] = near_ref[...].astype(F32)
        for frame in range(2):
            half = core if frame == 0 else 1 - core
            for b in range(nb):
                group = block_group(half, b, width, bw)
                far = far_ref[group].astype(F32)
                near = near_rows[pl.ds(group, 1), :]
                short = last = jnp.zeros((1, doubled), F32)
                for slot in range(slots):
                    is_last = lag_ref[group * slots + slot] == WIN - 1
                    taps = far[slot : slot + 1]
                    short = jnp.where(is_last, short, taps)
                    last = jnp.where(is_last, taps, last)
                near = jnp.concatenate([jnp.zeros((1, span), F32), near], axis=1)
                for at, taps in enumerate((near, short, last)):
                    matrix = skew(taps, span)
                    out_ref[1 - core, frame * nb + b, at] = matrix.astype(BF16)
                    out_ref[core, frame * nb + b, at] = matrix.T.astype(BF16)

    return call(
        body,
        "toeplitz",
        jax.ShapeDtypeStruct((2, 2 * nb, 3, span, span), BF16),
        [SMEM, VMEM, VMEM],
        VMEM,
        [pltpu.VMEM((groups, span), F32)],
    )(lags, far_taps, near_taps)


def outer(mixed, gated):
    return lax.dot_general(mixed, gated, (((1,), (1,)), ((), ())), preferred_element_type=F32)


def by_core(body):
    core = core_of()

    @pl.when(core == 0)
    def _():
        body(outer)

    @pl.when(core != 0)
    def _():
        body(lambda p, q: outer(q, p))


def correlate_near(p_own, q_own):
    span, hw = p_own[0].shape
    bw = min(GSIZE, hw)
    nb = hw // bw

    def body(p0, p1, q0, q1, rows_ref):
        def run(pair):
            for frame in range(2):
                for b in range(nb):
                    at = pl.ds(b * bw, bw)
                    matrix = pair((p0, p1)[frame][:, at], (q0, q1)[frame][:, at])
                    rows_ref[frame, pl.ds(b, 1), :] = diagonal_sums(matrix, span)

        by_core(run)

    return call(
        body,
        "correlate_near",
        jax.ShapeDtypeStruct((2, nb, 2 * span), F32),
        [VMEM] * 4,
        VMEM,
    )(*p_own, *q_own)


def correlate_far(lags, slots, near, p_own, q_own, r1, x0, x1, r2):
    span, hw = r2.shape
    bw = min(GSIZE, hw)
    nb = hw // bw

    def body(lag_ref, near_ref, p0, p1, q_ref, r1_ref, x0_ref, x10, x11, r2_ref, out_ref):
        core = core_of()

        def run(pair):
            for b in range(nb):
                at = pl.ds(b * bw, bw)
                p, x, r = p0[:, at], kept(x10[:, at], valid("Q", 2)), kept(r1_ref[:, at], valid("P", 1))
                is_one = short_lag(lag_ref, block_group(core, b, 2 * hw, bw), slots) == 1
                short = pair(jnp.where(is_one, r, p), jnp.where(is_one, q_ref[:, at], x))
                short += pair(p, jnp.where(is_one, x0_ref[:, at], jnp.zeros_like(p)))
                last = pair(r, x) + pair(p, kept(r2_ref[:, at], valid("Q", 3)))
                other = pair(p1[:, at], kept(x11[:, at], valid("Q", 2)))
                rows = [diagonal_sums(matrix, span) for matrix in (short, last, other)]
                empty = jnp.zeros_like(rows[0])
                for frame in range(2):
                    half = core if frame == 0 else 1 - core
                    group = block_group(half, b, 2 * hw, bw)
                    place = half * nb + b
                    if frame == 0:
                        close, distant = rows[0], rows[1]
                    else:
                        close = jnp.where(short_lag(lag_ref, group, slots) == 2, rows[2], empty)
                        distant = empty
                    out_ref[place, pl.ds(0, 1), :] = near_ref[frame, pl.ds(b, 1), :]
                    for slot in range(slots):
                        is_last = lag_ref[group * slots + slot] == WIN - 1
                        out_ref[place, pl.ds(1 + slot, 1), :] = jnp.where(is_last, distant, close)

        by_core(run)

    return call(
        body,
        "correlate_far",
        jax.ShapeDtypeStruct((2 * nb, slots + 1, 2 * span), F32),
        [SMEM] + [VMEM] * 9,
        VMEM,
    )(lags, near, *p_own, q_own[0], r1, x0, *x1, r2)


def near_sums(toeplitz, p_own, q_own):
    span, hw = p_own[0].shape
    bw = min(GSIZE, hw)
    nb = hw // bw

    def body(t_ref, p0, p1, q0, q1, out_ref):
        for role, panels in enumerate(((p0, p1), (q0, q1))):
            for frame in range(2):
                for b in range(nb):
                    at = pl.ds(b * bw, bw)
                    out_ref[role, frame, :, at] = jnp.dot(
                        t_ref[role, frame * nb + b, 0], panels[frame][:, at], preferred_element_type=F32
                    )

    return call(
        body,
        "near_sums",
        jax.ShapeDtypeStruct((2, 2, span, hw), F32),
        [VMEM] * 5,
        VMEM,
    )(toeplitz, *p_own, *q_own)


def partial_sums(lags, slots, toeplitz, sums, r1, x2, key, query):
    span, hw = r1[0].shape
    bw = min(GSIZE, hw)
    nb = hw // bw

    def body(lag_ref, t_ref, sums_ref, r10, r11, x20, x21, key_ref, query_ref, gate_ref, out_ref, sem):
        core = core_of()

        def load(ref):
            return pltpu.make_async_copy(ref, gate_ref, sem)

        @pl.when(core == 0)
        def _():
            load(query_ref).start()

        @pl.when(core != 0)
        def _():
            load(key_ref).start()

        for frame in range(2):
            half = core if frame == 0 else 1 - core
            for b in range(nb):
                at = pl.ds(b * bw, bw)
                group = block_group(half, b, 2 * hw, bw)
                is_one = short_lag(lag_ref, group, slots) == 1
                panel = jnp.where(is_one, (r10, r11)[frame][:, at], (x20, x21)[frame][:, at])
                panel = kept(panel, jnp.where(is_one, valid("P", 1), valid("P", 2)))
                total = sums_ref[0, frame, :, at]
                total += jnp.dot(t_ref[0, frame * nb + b, 1], panel, preferred_element_type=F32)
                out_ref[frame, :, at] = total
        load(key_ref).wait()

    return call(
        body,
        "partial_sums",
        [jax.ShapeDtypeStruct((span, 2 * hw), BF16), jax.ShapeDtypeStruct((2, span, hw), F32)],
        [SMEM] + [VMEM] * 6 + [HBM] * 2,
        [VMEM, VMEM],
        [pltpu.SemaphoreType.DMA],
    )(lags, toeplitz, sums, *r1, *x2, key, query)


def gated_output(role, panels, total_of, gates, results):
    span, width = gates[0].shape
    hw = width // 2
    bw = min(GSIZE, hw)
    nb = hw // bw
    role_at = 0 if role == "P" else 1
    count = len(panels)
    loads = len(gates) == 2

    def body(*refs):
        lag_ref, panel_refs, gate_refs = refs[0], refs[1:count], refs[count : count + len(gates)]
        block_ref, values_ref, held, sems = refs[-4 - loads : len(refs) - loads]
        core = core_of()
        to_block = core == role_at
        gate = refs[-1] if loads else gate_refs[0]

        def load(ref):
            return pltpu.make_async_copy(ref, gate, sems.at[2 * nb])

        def store(at, columns, ref):
            return pltpu.make_async_copy(held.at[at], ref.at[:, columns], sems.at[at])

        if loads:

            @pl.when(to_block)
            def _():
                load(gate_refs[1]).start()

            @pl.when(jnp.logical_not(to_block))
            def _():
                load(gate_refs[0]).start()

        for frame in range(2):
            half = core if frame == 0 else 1 - core
            for b in range(nb):
                at = frame * nb + b
                group = block_group(half, b, width, bw)
                total = total_of(lag_ref, group, frame, b, at, pl.ds(b * bw, bw), *panel_refs)
                if at == 0 and loads:
                    load(gate_refs[0]).wait()
                columns = pl.ds(pl.multiple_of(half * hw + b * bw, 128), bw)
                held[at] = (total * gate[:, columns].astype(F32)).astype(BF16)

                @pl.when(to_block)
                def _():
                    store(at, columns, block_ref).start()

                @pl.when(jnp.logical_not(to_block))
                def _():
                    store(at, columns, values_ref).start()

        for at in range(2 * nb):
            store(at, pl.ds(0, bw), block_ref).wait()

    shape = jax.ShapeDtypeStruct((span, width), BF16)
    scratch = [pltpu.VMEM((2 * nb, span, bw), BF16), pltpu.SemaphoreType.DMA((2 * nb + 1,))]
    if loads:
        scratch.append(pltpu.VMEM((span, width), BF16))
    first = count + len(gates)
    return call(
        body,
        f"out_{role.lower()}",
        [shape, shape],
        [SMEM] + [VMEM] * (count - 1) + [HBM if loads else VMEM] * len(gates) + [HBM] * len(results),
        [HBM, HBM],
        scratch,
        {first: 0, first + 1: 1} if results else None,
        flops=Q_OUTPUT_FLOPS if role == "Q" else 1,
    )(*panels, *gates, *results)


def q_output(lags, slots, toeplitz, sums, x0, x1, r2, key, query):
    def total_of(lag_ref, group, frame, b, place, at, t_ref, sums_ref, x00, x01, x10, x11, r20, r21):
        is_one = short_lag(lag_ref, group, slots) == 1
        panel = jnp.where(is_one, (x00, x01)[frame][:, at], (x10, x11)[frame][:, at])
        panel = kept(panel, jnp.logical_or(is_one, valid("Q", 2)))
        last = kept((r20, r21)[frame][:, at], valid("Q", 3))
        total = sums_ref[1, frame, :, at]
        total += jnp.dot(t_ref[1, place, 1], panel, preferred_element_type=F32)
        return total + jnp.dot(t_ref[1, place, 2], last, preferred_element_type=F32)

    return gated_output("Q", (lags, toeplitz, sums, *x0, *x1, *r2), total_of, (key, query), ())


def p_output(lags, toeplitz, sums, r3, gate, results):
    def total_of(lag_ref, group, frame, b, place, at, t_ref, sums_ref, r3_ref):
        last = jnp.dot(t_ref[0, place, 2], kept(r3_ref[frame, :, at], valid("P", 3)), preferred_element_type=F32)
        return sums_ref[frame, :, at] + last

    return gated_output("P", (lags, toeplitz, sums, r3), total_of, (gate,), results)


def after(value, *others):
    return lax.optimization_barrier((value,) + others)[0]


def stacked(parts):
    def body(*refs):
        for i, ref in enumerate(refs[:-1]):
            refs[-1][i] = ref[...]

    shape = jax.ShapeDtypeStruct((len(parts),) + parts[0].shape, parts[0].dtype)
    return call(body, "stack", shape, [VMEM] * len(parts), VMEM)(*parts)


def added(parts):
    def body(*refs):
        terms = [ref[...] for ref in refs[:-1]]
        while len(terms) > 1:
            terms = [a + b for a, b in zip(terms[::2], terms[1::2])]
        refs[-1][...] = terms[0]

    shape = jax.ShapeDtypeStruct(parts[0].shape, F32)
    return call(body, "add_rows", shape, [VMEM] * len(parts), VMEM)(*parts)


def sum_over_chips(rows):
    count = lax.axis_size("ctx")
    if count & (count - 1):
        return lax.psum(rows, "ctx")
    bit = 2
    while bit < count:
        steps = [k * bit for k in (3, 2, 1) if k * bit < count]
        others = [lax.ppermute(rows, "ctx", [(i, i ^ step) for i in range(count)]) for step in steps]
        rows = added(others + [rows])
        bit *= 4
    return rows


def sum_over_cores(rows):
    count = lax.axis_size("ctx")
    if count & (count - 1):
        return rows
    return added([rows, lax.ppermute(rows, "ctx", [(i, i ^ 1) for i in range(count)])])


def joined(first, second, bit):
    def body(first_ref, second_ref, out_ref):
        length = first_ref.shape[0]
        here = lax.rem(lax.div(lax.axis_index("chan"), bit), 2)
        out_ref[pl.ds(here * length, length)] = first_ref[...]
        out_ref[pl.ds((1 - here) * length, length)] = second_ref[...]

    shape = jax.ShapeDtypeStruct((2 * first.shape[0],) + first.shape[1:], F32)
    return call(body, "join_rows", shape, [VMEM] * 2, VMEM)(first, second)


def gather_over_chan(rows, works):
    count = lax.axis_size("chan")
    if count & (count - 1):
        return lax.all_gather(rows, "chan", axis=0, tiled=True)
    bit = 1
    while bit < count:
        other = lax.ppermute(rows, "chan", [(i, i ^ bit) for i in range(count)])
        if works:
            other = after(other, works[0])
            works = works[1:]
        rows = joined(rows, other, bit)
        bit *= 2
    return rows


def filter_gradients(rows, groups, span, scale):
    _, rows_per, doubled = rows.shape
    slots = rows_per - 1
    repeat = rows.shape[0] // groups

    def body(rows_ref, far_ref, near_ref):
        for group in range(groups):
            total = rows_ref[group * repeat]
            for at in range(1, repeat):
                total = total + rows_ref[group * repeat + at]
            far_ref[group] = total[1:] * scale
            near_ref[pl.ds(group, 1), :] = total[:1, span:] * scale

    return call(
        body,
        "filter_gradients",
        [
            jax.ShapeDtypeStruct((groups, slots, doubled), F32),
            jax.ShapeDtypeStruct((groups, span), F32),
        ],
        [VMEM],
        [VMEM, VMEM],
    )(rows)


def per_device(
    key_stream, value_stream, query_stream, grad_out, distant_lag_taps, near_taps, lag_blocks
):
    span, width = key_stream.shape
    groups = distant_lag_taps.shape[0]
    count = lax.axis_size("ctx")
    hw = width // 2
    bw = min(GSIZE, hw)

    def along(moves):
        chans = lax.axis_size("chan")
        moves = [(a, b) for a, b in moves if 0 <= b < count]
        sources, targets = {a for a, _ in moves}, {b for _, b in moves}
        moves += [(a, a ^ 1) for a in targets - sources if (a ^ 1) in sources - targets]
        pairs = [(a * chans + c, b * chans + c) for a, b in moves for c in range(chans)]
        if chans % 2 == 0:
            idle = set(range(count)) - sources - targets
            pairs += [(a * chans + c, a * chans + (c ^ 1)) for a in sorted(idle) for c in range(chans)]
        return sorted(pairs)

    swap = along([(i, i ^ 1) for i in range(count)])
    to_near = along([(i, i + 1 if i % 2 else i - 1) for i in range(count)])
    to_far = along([(i, i - 3 if i % 2 else i + 3) for i in range(count)])
    onward = along([(i, i - 2 if i % 2 else i + 2) for i in range(count)])

    def send(value, moves):
        return lax.ppermute(value, ("ctx", "chan"), moves)

    slots = lag_blocks.shape[1]
    streams = (key_stream, value_stream, query_stream, grad_out)
    streams = tuple(pltpu.with_memory_space_constraint(x, pltpu.HBM) for x in streams)
    qa, qb = stream_products(("Q0", "Q1"), streams, "q_stream")
    r1a, r1b = send(qa, to_near), send(qb, to_near)
    *late, far_taps, near_taps, lags, _ = lax.optimization_barrier(
        streams + (distant_lag_taps, near_taps, lag_blocks, qb)
    )
    lags = lags.reshape(-1)
    pa, pb = stream_products(("P0", "P1"), late, "p_stream")
    q_own, p_own = (qb, qa), (pb, pa)
    toeplitz = toeplitz_matrices(lags, far_taps, near_taps, span, width, bw)
    near = correlate_near(p_own, q_own)

    sums = near_sums(toeplitz, p_own, q_own)

    r2a = send(after(pa, near, sums), to_far)
    r1 = lax.optimization_barrier(((r1a, r1b), sums, near))[0]
    x1 = (send(r1[1], swap), send(r1[0], swap))
    x0a = send(after(pa, r1), swap)
    r2b = send(after(pb, r1), to_far)
    both, r1 = lax.optimization_barrier((stacked(r1), r1))
    rows = correlate_far(lags, slots, near, p_own, q_own, r1[0], x0a, x1, r2a)
    r3 = send(after(both, rows), onward)
    rows = sum_over_cores(sum_over_chips(rows))
    pb_late, r2_late, rows = lax.optimization_barrier((pb, (r2a, r2b), rows))
    x0b = send(pb_late, swap)
    x2 = (send(r2_late[1], swap), send(r2_late[0], swap))
    gates = (key_stream, query_stream)
    results = q_output(lags, slots, toeplitz, sums, (x0a, x0b), x1, (r2a, r2b), *gates)
    gate, sums = partial_sums(lags, slots, toeplitz, sums, r1, x2, *gates)
    rows = gather_over_chan(rows, [results[0], sums])
    results = p_output(lags, toeplitz, sums, r3, gate, results)
    scale = 1.0 / math.sqrt(span * count * GSIZE)
    far, near = filter_gradients(rows, groups, span, scale)
    return (results[0], results[1], far, near)


def solution(mesh):
    streams = P("ctx", "chan")
    return jax.shard_map(
        per_device,
        mesh=mesh,
        in_specs=(streams, streams, streams, streams, P(), P(), P()),
        out_specs=(streams, streams, P(), P()),
        check_vma=False,
    )
```

```python
import functools
import math

import jax
import jax.numpy as jnp
from jax import lax
from jax.experimental import pallas as pl
from jax.experimental.pallas import tpu as pltpu
from jax.sharding import PartitionSpec as P

GSIZE = 512
WIN = 4
PARTIAL_SUMS_FLOPS = 52 * 10**8
VMEM_LIMIT = 16 * 1024 * 1024
BF16 = jnp.bfloat16
F32 = jnp.float32

VMEM = pl.BlockSpec(memory_space=pltpu.VMEM)
SMEM = pl.BlockSpec(memory_space=pltpu.SMEM)
HBM = pl.BlockSpec(memory_space=pltpu.HBM)


def core_of():
    return lax.rem(lax.axis_index("ctx"), 2)


def call(body, name, out_shape, in_specs, out_specs, scratch=(), aliases=None, limit=VMEM_LIMIT, flops=1):
    def run(*args):
        moved = sum(a.size * a.dtype.itemsize for a in args + tuple(jax.tree.leaves(out_shape)))
        return pl.pallas_call(
            body,
            in_specs=in_specs,
            out_specs=out_specs,
            out_shape=out_shape,
            scratch_shapes=scratch,
            input_output_aliases=aliases or {},
            compiler_params=pltpu.CompilerParams(vmem_limit_bytes=limit),
            cost_estimate=pl.CostEstimate(flops=flops, bytes_accessed=moved, transcendentals=0),
            name=name,
        )(*args)

    return run


def valid(stream, lag):
    place = lax.axis_index("ctx")
    earlier, later = place >= lag, place + lag < lax.axis_size("ctx")
    return jnp.where(core_of() == (0 if stream == "P" else 1), earlier, later)


def kept(panel, exists):
    return jnp.where(exists, panel, jnp.zeros_like(panel))


def block_group(half, block, width, bw):
    first = lax.axis_index("chan") * width + half * (width // 2) + block * bw
    return lax.div(first, GSIZE)


def rolled(value, shift):
    shift %= value.shape[1]
    if shift % 128 == 0:
        return value if shift == 0 else jnp.concatenate([value[:, -shift:], value[:, :-shift]], axis=1)
    return pltpu.roll(value, shift, 1)


def skew(taps, span):
    width = 2 * span
    row = rolled(jnp.broadcast_to(taps, (8, width)), span)
    index = lax.broadcasted_iota(jnp.int32, (8, width), 0)
    for bit in (1, 2, 4):
        row = jnp.where((index & bit) != 0, rolled(row, bit), row)
    filled = 8
    while filled < span:
        row = jnp.concatenate([row, rolled(row, filled)], axis=0)
        filled *= 2
    return row[:, :span]


def diagonal_sums(matrix, span):
    width = 2 * span
    rows = jnp.concatenate([matrix, jnp.zeros((span, span), F32)], axis=1)
    half = span // 2
    while half >= 8:
        rows = rows[:half] + rolled(rows[half:], -half)
        half //= 2
    index = lax.broadcasted_iota(jnp.int32, (8, width), 0)
    for bit in (1, 2, 4):
        rows = jnp.where((index & bit) != 0, rolled(rows, -bit), rows)
    return rolled(jnp.sum(rows, axis=0, keepdims=True), span)


def stream_products(wanted, streams, name):
    span, width = streams[0].shape
    hw = width // 2
    count = len(wanted)

    def body(k_ref, v_ref, q_ref, g_ref, *rest):
        outs, (held, sems) = rest[:-2], rest[-2:]
        core = core_of()

        def copies(at, pair):
            half = 1 - core if wanted[at][1] == "0" else core
            columns = pl.ds(pl.multiple_of(half * hw, 128), hw)
            return [
                pltpu.make_async_copy(ref.at[:, columns], held.at[at, i], sems.at[at, i])
                for i, ref in enumerate(pair)
            ]

        for at, kind in enumerate(wanted):
            mixed_core = 0 if kind[0] == "P" else 1
            for is_mixed, pair in ((True, (k_ref, v_ref)), (False, (g_ref, q_ref))):

                @pl.when((core == mixed_core) == is_mixed)
                def _():
                    for copy in copies(at, pair):
                        copy.start()

        for at in range(count):
            for copy in copies(at, (k_ref, v_ref)):
                copy.wait()
            product = (held[at, 0].astype(F32) * held[at, 1].astype(F32)).astype(BF16)
            outs[at][...] = product

    return call(
        body,
        name,
        [jax.ShapeDtypeStruct((span, hw), BF16)] * count,
        [HBM] * 4,
        [VMEM] * count,
        [pltpu.VMEM((count, 2, span, hw), BF16), pltpu.SemaphoreType.DMA((count, 2))],
    )(*streams)


def short_lag(lag_ref, group, slots):
    lag = lag_ref[group * slots]
    for slot in range(1, slots):
        lag = jnp.minimum(lag, lag_ref[group * slots + slot])
    return lag


def toeplitz_matrices(lags, far_taps, near_taps, span, width, bw):
    groups, slots, doubled = far_taps.shape
    nb = width // 2 // bw

    def body(lag_ref, far_ref, near_ref, out_ref, near_rows):
        core = core_of()
        near_rows[...] = near_ref[...].astype(F32)
        for frame in range(2):
            half = core if frame == 0 else 1 - core
            for b in range(nb):
                group = block_group(half, b, width, bw)
                far = far_ref[group].astype(F32)
                near = near_rows[pl.ds(group, 1), :]
                short = last = jnp.zeros((1, doubled), F32)
                for slot in range(slots):
                    is_last = lag_ref[group * slots + slot] == WIN - 1
                    taps = far[slot : slot + 1]
                    short = jnp.where(is_last, short, taps)
                    last = jnp.where(is_last, taps, last)
                near = jnp.concatenate([jnp.zeros((1, span), F32), near], axis=1)
                for at, taps in enumerate((near, short, last)):
                    matrix = skew(taps, span)
                    out_ref[1 - core, frame * nb + b, at] = matrix.astype(BF16)
                    out_ref[core, frame * nb + b, at] = matrix.T.astype(BF16)

    return call(
        body,
        "toeplitz",
        jax.ShapeDtypeStruct((2, 2 * nb, 3, span, span), BF16),
        [SMEM, VMEM, VMEM],
        VMEM,
        [pltpu.VMEM((groups, span), F32)],
    )(lags, far_taps, near_taps)


def outer(mixed, gated):
    return lax.dot_general(mixed, gated, (((1,), (1,)), ((), ())), preferred_element_type=F32)


def by_core(body):
    core = core_of()

    @pl.when(core == 0)
    def _():
        body(outer)

    @pl.when(core != 0)
    def _():
        body(lambda p, q: outer(q, p))


def correlate_near(p_own, q_own):
    span, hw = p_own[0].shape
    bw = min(GSIZE, hw)
    nb = hw // bw

    def body(p0, p1, q0, q1, rows_ref):
        def run(pair):
            for frame in range(2):
                for b in range(nb):
                    at = pl.ds(b * bw, bw)
                    matrix = pair((p0, p1)[frame][:, at], (q0, q1)[frame][:, at])
                    rows_ref[frame, pl.ds(b, 1), :] = diagonal_sums(matrix, span)

        by_core(run)

    return call(
        body,
        "correlate_near",
        jax.ShapeDtypeStruct((2, nb, 2 * span), F32),
        [VMEM] * 4,
        VMEM,
    )(*p_own, *q_own)


def correlate_far(lags, slots, near, p_own, q_own, r1, x0, x1, r2):
    span, hw = r2.shape
    bw = min(GSIZE, hw)
    nb = hw // bw

    def body(lag_ref, near_ref, p0, p1, q_ref, r1_ref, x0_ref, x10, x11, r2_ref, out_ref):
        core = core_of()

        def run(pair):
            for b in range(nb):
                at = pl.ds(b * bw, bw)
                p, x, r = p0[:, at], kept(x10[:, at], valid("Q", 2)), kept(r1_ref[:, at], valid("P", 1))
                is_one = short_lag(lag_ref, block_group(core, b, 2 * hw, bw), slots) == 1
                short = pair(jnp.where(is_one, r, p), jnp.where(is_one, q_ref[:, at], x))
                short += pair(p, jnp.where(is_one, x0_ref[:, at], jnp.zeros_like(p)))
                last = pair(r, x) + pair(p, kept(r2_ref[:, at], valid("Q", 3)))
                other = pair(p1[:, at], kept(x11[:, at], valid("Q", 2)))
                rows = [diagonal_sums(matrix, span) for matrix in (short, last, other)]
                empty = jnp.zeros_like(rows[0])
                for frame in range(2):
                    half = core if frame == 0 else 1 - core
                    group = block_group(half, b, 2 * hw, bw)
                    place = half * nb + b
                    if frame == 0:
                        close, distant = rows[0], rows[1]
                    else:
                        close = jnp.where(short_lag(lag_ref, group, slots) == 2, rows[2], empty)
                        distant = empty
                    out_ref[place, pl.ds(0, 1), :] = near_ref[frame, pl.ds(b, 1), :]
                    for slot in range(slots):
                        is_last = lag_ref[group * slots + slot] == WIN - 1
                        out_ref[place, pl.ds(1 + slot, 1), :] = jnp.where(is_last, distant, close)

        by_core(run)

    return call(
        body,
        "correlate_far",
        jax.ShapeDtypeStruct((2 * nb, slots + 1, 2 * span), F32),
        [SMEM] + [VMEM] * 9,
        VMEM,
    )(lags, near, *p_own, q_own[0], r1, x0, *x1, r2)


def near_sums(toeplitz, p_own, q_own, key, query):
    span, hw = p_own[0].shape
    bw = min(GSIZE, hw)
    nb = hw // bw

    def body(t_ref, p0, p1, q0, q1, key_ref, query_ref, out_ref, p_gate, q_gate, sems):
        core = core_of()

        def loads(first, second):
            return (
                pltpu.make_async_copy(first, p_gate, sems.at[0]),
                pltpu.make_async_copy(second, q_gate, sems.at[1]),
            )

        for number, refs in ((0, (query_ref, key_ref)), (1, (key_ref, query_ref))):

            @pl.when(core == number)
            def _():
                for load in loads(*refs):
                    load.start()

        for role, panels in enumerate(((p0, p1), (q0, q1))):
            for frame in range(2):
                for b in range(nb):
                    at = pl.ds(b * bw, bw)
                    out_ref[role, frame, :, at] = jnp.dot(
                        t_ref[role, frame * nb + b, 0], panels[frame][:, at], preferred_element_type=F32
                    )
        for load in loads(key_ref, query_ref):
            load.wait()

    gate = jax.ShapeDtypeStruct((span, 2 * hw), BF16)
    return call(
        body,
        "near_sums",
        [jax.ShapeDtypeStruct((2, 2, span, hw), F32), gate, gate],
        [VMEM] * 5 + [HBM] * 2,
        [VMEM] * 3,
        [pltpu.SemaphoreType.DMA((2,))],
    )(toeplitz, *p_own, *q_own, key, query)


def partial_sums(lags, slots, toeplitz, sums, r1, x2):
    span, hw = r1[0].shape
    bw = min(GSIZE, hw)
    nb = hw // bw

    def body(lag_ref, t_ref, sums_ref, r10, r11, x20, x21, out_ref):
        core = core_of()
        for frame in range(2):
            half = core if frame == 0 else 1 - core
            for b in range(nb):
                at = pl.ds(b * bw, bw)
                group = block_group(half, b, 2 * hw, bw)
                is_one = short_lag(lag_ref, group, slots) == 1
                panel = jnp.where(is_one, (r10, r11)[frame][:, at], (x20, x21)[frame][:, at])
                panel = kept(panel, jnp.where(is_one, valid("P", 1), valid("P", 2)))
                total = sums_ref[0, frame, :, at]
                total += jnp.dot(t_ref[0, frame * nb + b, 1], panel, preferred_element_type=F32)
                out_ref[frame, :, at] = total

    return call(
        body,
        "partial_sums",
        jax.ShapeDtypeStruct((2, span, hw), F32),
        [SMEM] + [VMEM] * 6,
        VMEM,
        flops=PARTIAL_SUMS_FLOPS,
    )(lags, toeplitz, sums, *r1, *x2)


def gated_output(role, frames, panels, total_of, gate, results):
    span, width = gate.shape
    hw = width // 2
    bw = min(GSIZE, hw)
    nb = hw // bw
    role_at = 0 if role == "P" else 1
    count = len(panels)

    def body(*refs):
        lag_ref, panel_refs, gate_ref = refs[0], refs[1:count], refs[count]
        block_ref, values_ref, held, sems = refs[-4:]
        core = core_of()
        to_block = core == role_at

        def store(at, columns, ref):
            return pltpu.make_async_copy(held.at[at], ref.at[:, columns], sems.at[at])

        for at in range(len(frames) * nb):
            frame, b = frames[at // nb], at % nb
            half = core if frame == 0 else 1 - core
            group = block_group(half, b, width, bw)
            total = total_of(lag_ref, group, frame, frame * nb + b, pl.ds(b * bw, bw), *panel_refs)
            columns = pl.ds(pl.multiple_of(half * hw + b * bw, 128), bw)
            held[at] = (total * gate_ref[:, columns].astype(F32)).astype(BF16)

            @pl.when(to_block)
            def _():
                store(at, columns, block_ref).start()

            @pl.when(jnp.logical_not(to_block))
            def _():
                store(at, columns, values_ref).start()

        for at in range(len(frames) * nb):
            store(at, pl.ds(0, bw), block_ref).wait()

    shape = jax.ShapeDtypeStruct((span, width), BF16)
    return call(
        body,
        f"out_{role.lower()}" + "".join(map(str, frames)),
        [shape, shape],
        [SMEM] + [VMEM] * count + [HBM] * len(results),
        [HBM, HBM],
        [
            pltpu.VMEM((len(frames) * nb, span, bw), BF16),
            pltpu.SemaphoreType.DMA((len(frames) * nb,)),
        ],
        {count + 1: 0, count + 2: 1} if results else None,
    )(*panels, gate, *results)


def q_output(frame, lags, slots, toeplitz, sums, x0, x1, r2, gate, results):
    def total_of(lag_ref, group, frame, place, at, t_ref, sums_ref, x0_ref, x1_ref, r2_ref):
        is_one = short_lag(lag_ref, group, slots) == 1
        panel = kept(jnp.where(is_one, x0_ref[:, at], x1_ref[:, at]), jnp.logical_or(is_one, valid("Q", 2)))
        last = kept(r2_ref[:, at], valid("Q", 3))
        total = sums_ref[1, frame, :, at]
        total += jnp.dot(t_ref[1, place, 1], panel, preferred_element_type=F32)
        return total + jnp.dot(t_ref[1, place, 2], last, preferred_element_type=F32)

    return gated_output("Q", (frame,), (lags, toeplitz, sums, x0, x1, r2), total_of, gate, results)


def p_output(lags, toeplitz, sums, r3, gate, results):
    def total_of(lag_ref, group, frame, place, at, t_ref, sums_ref, r3_ref):
        last = kept(r3_ref[frame, :, at], valid("P", 3))
        return sums_ref[frame, :, at] + jnp.dot(t_ref[0, place, 2], last, preferred_element_type=F32)

    return gated_output("P", (0, 1), (lags, toeplitz, sums, r3), total_of, gate, results)


def after(value, *others):
    return lax.optimization_barrier((value,) + others)[0]


def stacked(parts):
    def body(*refs):
        for i, ref in enumerate(refs[:-1]):
            refs[-1][i] = ref[...]

    shape = jax.ShapeDtypeStruct((len(parts),) + parts[0].shape, parts[0].dtype)
    return call(body, "stack", shape, [VMEM] * len(parts), VMEM)(*parts)


def added(parts):
    def body(*refs):
        terms = [ref[...] for ref in refs[:-1]]
        while len(terms) > 1:
            terms = [a + b for a, b in zip(terms[::2], terms[1::2])]
        refs[-1][...] = terms[0]

    shape = jax.ShapeDtypeStruct(parts[0].shape, F32)
    return call(body, "add_rows", shape, [VMEM] * len(parts), VMEM)(*parts)


def sum_over_chips(rows, work):
    count = lax.axis_size("ctx")
    if count & (count - 1):
        return lax.psum(rows, "ctx")
    bit = 2
    while bit < count:
        steps = [k * bit for k in (3, 2, 1) if k * bit < count]
        others = [lax.ppermute(rows, "ctx", [(i, i ^ step) for i in range(count)]) for step in steps]
        if bit == 2:
            others = list(lax.optimization_barrier((*others, work))[:-1])
        if len(others) == 3:
            farthest = added(others[:1])
            others = [farthest] + list(lax.optimization_barrier((others[1], others[2], farthest))[:2])
        rows = added(others + [rows])
        bit *= 4
    return rows


def sum_over_cores(rows):
    count = lax.axis_size("ctx")
    if count & (count - 1):
        return rows
    return added([rows, lax.ppermute(rows, "ctx", [(i, i ^ 1) for i in range(count)])])


def joined(first, second, bit):
    def body(first_ref, second_ref, out_ref):
        length = first_ref.shape[0]
        here = lax.rem(lax.div(lax.axis_index("chan"), bit), 2)
        out_ref[pl.ds(here * length, length)] = first_ref[...]
        out_ref[pl.ds((1 - here) * length, length)] = second_ref[...]

    shape = jax.ShapeDtypeStruct((2 * first.shape[0],) + first.shape[1:], F32)
    return call(body, "join_rows", shape, [VMEM] * 2, VMEM)(first, second)


def crossed(bit):
    ctxs, chans = lax.axis_size("ctx"), lax.axis_size("chan")
    core = 1 if ctxs % 2 == 0 else 0
    return [(i * chans + c, (i ^ core) * chans + (c ^ bit)) for i in range(ctxs) for c in range(chans)]


def gather_over_chan(rows, works):
    count = lax.axis_size("chan")
    if count & (count - 1):
        return lax.all_gather(rows, "chan", axis=0, tiled=True), None
    bit, other = 1, None
    while bit < count:
        if other is not None:
            rows = joined(rows, other, bit // 2)
        other = lax.ppermute(rows, ("ctx", "chan"), crossed(bit))
        if works:
            other = after(other, works[0])
            works = works[1:]
        bit *= 2
    return rows, other


def filter_gradients(rows, other, groups, span, scale):
    blocks, rows_per, doubled = rows.shape
    slots = rows_per - 1
    lists = [rows] if other is None else [rows, other]
    repeat = len(lists) * blocks // groups
    count = lax.axis_size("chan")

    def body(*refs):
        far_ref, near_ref = refs[-2:]
        upper = lax.div(2 * lax.axis_index("chan"), count) if len(lists) == 2 else 0
        for at in range(0, len(lists) * blocks, repeat):
            source = refs[at // blocks]
            total = source[at % blocks]
            for more in range(at % blocks + 1, at % blocks + repeat):
                total = total + source[more]
            place = at // repeat
            if len(lists) == 2:
                place = lax.rem(place + upper * (groups // 2), groups)
            far_ref[place] = total[1:] * scale
            near_ref[pl.ds(place, 1), :] = total[:1, span:] * scale

    return call(
        body,
        "filter_gradients",
        [
            jax.ShapeDtypeStruct((groups, slots, doubled), F32),
            jax.ShapeDtypeStruct((groups, span), F32),
        ],
        [VMEM] * len(lists),
        [VMEM, VMEM],
    )(*lists)


def per_device(
    key_stream, value_stream, query_stream, grad_out, distant_lag_taps, near_taps, lag_blocks
):
    span, width = key_stream.shape
    groups = distant_lag_taps.shape[0]
    count = lax.axis_size("ctx")
    hw = width // 2
    bw = min(GSIZE, hw)

    def along(moves):
        chans = lax.axis_size("chan")
        moves = [(a, b) for a, b in moves if 0 <= b < count]
        sources, targets = {a for a, _ in moves}, {b for _, b in moves}
        moves += [(a, a ^ 1) for a in targets - sources if (a ^ 1) in sources - targets]
        pairs = [(a * chans + c, b * chans + c) for a, b in moves for c in range(chans)]
        if chans % 2 == 0:
            idle = set(range(count)) - sources - targets
            pairs += [(a * chans + c, a * chans + (c ^ 1)) for a in sorted(idle) for c in range(chans)]
        return sorted(pairs)

    swap = along([(i, i ^ 1) for i in range(count)])
    to_near = along([(i, i + 1 if i % 2 else i - 1) for i in range(count)])
    to_far = along([(i, i - 3 if i % 2 else i + 3) for i in range(count)])
    onward = along([(i, i - 2 if i % 2 else i + 2) for i in range(count)])

    def send(value, moves):
        return lax.ppermute(value, ("ctx", "chan"), moves)

    slots = lag_blocks.shape[1]
    streams = (key_stream, value_stream, query_stream, grad_out)
    streams = tuple(pltpu.with_memory_space_constraint(x, pltpu.HBM) for x in streams)
    qa, qb = stream_products(("Q0", "Q1"), streams, "q_stream")
    r1a, r1b = send(qa, to_near), send(qb, to_near)
    *late, far_taps, near_taps, lags, _ = lax.optimization_barrier(
        streams + (distant_lag_taps, near_taps, lag_blocks, qb)
    )
    lags = lags.reshape(-1)
    pa, pb = stream_products(("P0", "P1"), late, "p_stream")
    q_own, p_own = (qb, qa), (pb, pa)
    toeplitz = toeplitz_matrices(lags, far_taps, near_taps, span, width, bw)
    near = correlate_near(p_own, q_own)

    sums, p_gate, q_gate = near_sums(toeplitz, p_own, q_own, streams[0], streams[2])

    r2a = send(after(pa, near, sums), to_far)
    r1 = lax.optimization_barrier(((r1a, r1b), sums, near))[0]
    x1 = (send(r1[1], swap), send(r1[0], swap))
    x0a = send(after(pa, r1), swap)
    r2b = send(after(pb, r1), to_far)
    both, r1 = lax.optimization_barrier((stacked(r1), r1))
    rows = correlate_far(lags, slots, near, p_own, q_own, r1[0], x0a, x1, r2a)
    r3 = send(after(both, rows), onward)
    q_sums, pb_late, r2b, _ = lax.optimization_barrier((sums, pb, r2b, rows))
    results = q_output(0, lags, slots, toeplitz, q_sums, x0a, x1[0], r2a, q_gate, ())
    x0b = send(after(pb_late, r2b), swap)
    rows = sum_over_cores(sum_over_chips(rows, results[0]))
    r2_late, rows = lax.optimization_barrier(((r2a, r2b), rows))
    x2 = (send(r2_late[1], swap), send(r2_late[0], swap))
    results = q_output(1, lags, slots, toeplitz, sums, x0b, x1[1], r2b, q_gate, results)
    sums = partial_sums(lags, slots, toeplitz, sums, r1, x2)
    rows, other = gather_over_chan(rows, [results[0], sums])
    scale = 1.0 / math.sqrt(span * count * GSIZE)
    far, near = filter_gradients(rows, other, groups, span, scale)
    results = p_output(lags, toeplitz, sums, r3, p_gate, results)
    return (results[0], results[1], far, near)


def solution(mesh):
    streams = P("ctx", "chan")
    return jax.shard_map(
        per_device,
        mesh=mesh,
        in_specs=(streams, streams, streams, streams, P(), P(), P()),
        out_specs=(streams, streams, P(), P()),
        check_vma=False,
    )
```

```python
import functools
import math

import jax
import jax.numpy as jnp
from jax import lax
from jax.experimental import pallas as pl
from jax.experimental.pallas import tpu as pltpu
from jax.sharding import PartitionSpec as P

GSIZE = 512
WIN = 4
PARTIAL_SUMS_FLOPS = 52 * 10**8
VMEM_LIMIT = 16 * 1024 * 1024
BF16 = jnp.bfloat16
F32 = jnp.float32

VMEM = pl.BlockSpec(memory_space=pltpu.VMEM)
SMEM = pl.BlockSpec(memory_space=pltpu.SMEM)
HBM = pl.BlockSpec(memory_space=pltpu.HBM)


def core_of():
    return lax.rem(lax.axis_index("ctx"), 2)


def call(body, name, out_shape, in_specs, out_specs, scratch=(), aliases=None, limit=VMEM_LIMIT, flops=1):
    def run(*args):
        moved = sum(a.size * a.dtype.itemsize for a in args + tuple(jax.tree.leaves(out_shape)))
        return pl.pallas_call(
            body,
            in_specs=in_specs,
            out_specs=out_specs,
            out_shape=out_shape,
            scratch_shapes=scratch,
            input_output_aliases=aliases or {},
            compiler_params=pltpu.CompilerParams(vmem_limit_bytes=limit),
            cost_estimate=pl.CostEstimate(flops=flops, bytes_accessed=moved, transcendentals=0),
            name=name,
        )(*args)

    return run


def valid(stream, lag):
    place = lax.axis_index("ctx")
    earlier, later = place >= lag, place + lag < lax.axis_size("ctx")
    return jnp.where(core_of() == (0 if stream == "P" else 1), earlier, later)


def kept(panel, exists):
    return jnp.where(exists, panel, jnp.zeros_like(panel))


def block_group(half, block, width, bw):
    first = lax.axis_index("chan") * width + half * (width // 2) + block * bw
    return lax.div(first, GSIZE)


def rolled(value, shift):
    shift %= value.shape[1]
    if shift % 128 == 0:
        return value if shift == 0 else jnp.concatenate([value[:, -shift:], value[:, :-shift]], axis=1)
    return pltpu.roll(value, shift, 1)


def skew(taps, span):
    width = 2 * span
    row = rolled(jnp.broadcast_to(taps, (8, width)), span)
    index = lax.broadcasted_iota(jnp.int32, (8, width), 0)
    for bit in (1, 2, 4):
        row = jnp.where((index & bit) != 0, rolled(row, bit), row)
    filled = 8
    while filled < span:
        row = jnp.concatenate([row, rolled(row, filled)], axis=0)
        filled *= 2
    return row[:, :span]


def diagonal_sums(matrix, span):
    width = 2 * span
    rows = jnp.concatenate([matrix, jnp.zeros((span, span), F32)], axis=1)
    half = span // 2
    while half >= 8:
        rows = rows[:half] + rolled(rows[half:], -half)
        half //= 2
    index = lax.broadcasted_iota(jnp.int32, (8, width), 0)
    for bit in (1, 2, 4):
        rows = jnp.where((index & bit) != 0, rolled(rows, -bit), rows)
    return rolled(jnp.sum(rows, axis=0, keepdims=True), span)


def stream_products(wanted, streams, name):
    span, width = streams[0].shape
    hw = width // 2
    count = len(wanted)

    def body(k_ref, v_ref, q_ref, g_ref, *rest):
        outs, (held, sems) = rest[:-2], rest[-2:]
        core = core_of()

        def copies(at, pair):
            half = 1 - core if wanted[at][1] == "0" else core
            columns = pl.ds(pl.multiple_of(half * hw, 128), hw)
            return [
                pltpu.make_async_copy(ref.at[:, columns], held.at[at, i], sems.at[at, i])
                for i, ref in enumerate(pair)
            ]

        for at, kind in enumerate(wanted):
            mixed_core = 0 if kind[0] == "P" else 1
            for is_mixed, pair in ((True, (k_ref, v_ref)), (False, (g_ref, q_ref))):

                @pl.when((core == mixed_core) == is_mixed)
                def _():
                    for copy in copies(at, pair):
                        copy.start()

        for at in range(count):
            for copy in copies(at, (k_ref, v_ref)):
                copy.wait()
            product = (held[at, 0].astype(F32) * held[at, 1].astype(F32)).astype(BF16)
            outs[at][...] = product

    return call(
        body,
        name,
        [jax.ShapeDtypeStruct((span, hw), BF16)] * count,
        [HBM] * 4,
        [VMEM] * count,
        [pltpu.VMEM((count, 2, span, hw), BF16), pltpu.SemaphoreType.DMA((count, 2))],
    )(*streams)


def short_lag(lag_ref, group, slots):
    lag = lag_ref[group * slots]
    for slot in range(1, slots):
        lag = jnp.minimum(lag, lag_ref[group * slots + slot])
    return lag


def toeplitz_matrices(lags, far_taps, near_taps, span, width, bw):
    groups, slots, doubled = far_taps.shape
    nb = width // 2 // bw

    def body(lag_ref, far_ref, near_ref, out_ref, near_rows):
        core = core_of()
        near_rows[...] = near_ref[...].astype(F32)
        for frame in range(2):
            half = core if frame == 0 else 1 - core
            for b in range(nb):
                group = block_group(half, b, width, bw)
                far = far_ref[group].astype(F32)
                near = near_rows[pl.ds(group, 1), :]
                short = last = jnp.zeros((1, doubled), F32)
                for slot in range(slots):
                    is_last = lag_ref[group * slots + slot] == WIN - 1
                    taps = far[slot : slot + 1]
                    short = jnp.where(is_last, short, taps)
                    last = jnp.where(is_last, taps, last)
                near = jnp.concatenate([jnp.zeros((1, span), F32), near], axis=1)
                for at, taps in enumerate((near, short, last)):
                    matrix = skew(taps, span)
                    out_ref[1 - core, frame * nb + b, at] = matrix.astype(BF16)
                    out_ref[core, frame * nb + b, at] = matrix.T.astype(BF16)

    return call(
        body,
        "toeplitz",
        jax.ShapeDtypeStruct((2, 2 * nb, 3, span, span), BF16),
        [SMEM, VMEM, VMEM],
        VMEM,
        [pltpu.VMEM((groups, span), F32)],
    )(lags, far_taps, near_taps)


def outer(mixed, gated):
    return lax.dot_general(mixed, gated, (((1,), (1,)), ((), ())), preferred_element_type=F32)


def by_core(body):
    core = core_of()

    @pl.when(core == 0)
    def _():
        body(outer)

    @pl.when(core != 0)
    def _():
        body(lambda p, q: outer(q, p))


def correlate_near(p_own, q_own):
    span, hw = p_own[0].shape
    bw = min(GSIZE, hw)
    nb = hw // bw

    def body(p0, p1, q0, q1, rows_ref):
        def run(pair):
            for frame in range(2):
                for b in range(nb):
                    at = pl.ds(b * bw, bw)
                    matrix = pair((p0, p1)[frame][:, at], (q0, q1)[frame][:, at])
                    rows_ref[frame, pl.ds(b, 1), :] = diagonal_sums(matrix, span)

        by_core(run)

    return call(
        body,
        "correlate_near",
        jax.ShapeDtypeStruct((2, nb, 2 * span), F32),
        [VMEM] * 4,
        VMEM,
    )(*p_own, *q_own)


def correlate_far(lags, slots, near, p_own, q_own, r1, x0, x1, r2):
    span, hw = r2.shape
    bw = min(GSIZE, hw)
    nb = hw // bw

    def body(lag_ref, near_ref, p0, p1, q_ref, r1_ref, x0_ref, x10, x11, r2_ref, out_ref):
        core = core_of()

        def run(pair):
            for b in range(nb):
                at = pl.ds(b * bw, bw)
                p, x, r = p0[:, at], kept(x10[:, at], valid("Q", 2)), kept(r1_ref[:, at], valid("P", 1))
                is_one = short_lag(lag_ref, block_group(core, b, 2 * hw, bw), slots) == 1
                short = pair(jnp.where(is_one, r, p), jnp.where(is_one, q_ref[:, at], x))
                short += pair(p, jnp.where(is_one, x0_ref[:, at], jnp.zeros_like(p)))
                last = pair(r, x) + pair(p, kept(r2_ref[:, at], valid("Q", 3)))
                other = pair(p1[:, at], kept(x11[:, at], valid("Q", 2)))
                rows = [diagonal_sums(matrix, span) for matrix in (short, last, other)]
                empty = jnp.zeros_like(rows[0])
                for frame in range(2):
                    half = core if frame == 0 else 1 - core
                    group = block_group(half, b, 2 * hw, bw)
                    place = half * nb + b
                    if frame == 0:
                        close, distant = rows[0], rows[1]
                    else:
                        close = jnp.where(short_lag(lag_ref, group, slots) == 2, rows[2], empty)
                        distant = empty
                    out_ref[place, pl.ds(0, 1), :] = near_ref[frame, pl.ds(b, 1), :]
                    for slot in range(slots):
                        is_last = lag_ref[group * slots + slot] == WIN - 1
                        out_ref[place, pl.ds(1 + slot, 1), :] = jnp.where(is_last, distant, close)

        by_core(run)

    return call(
        body,
        "correlate_far",
        jax.ShapeDtypeStruct((2 * nb, slots + 1, 2 * span), F32),
        [SMEM] + [VMEM] * 9,
        VMEM,
    )(lags, near, *p_own, q_own[0], r1, x0, *x1, r2)


def near_sums(toeplitz, p_own, q_own, key, query):
    span, hw = p_own[0].shape
    bw = min(GSIZE, hw)
    nb = hw // bw

    def body(t_ref, p0, p1, q0, q1, key_ref, query_ref, out_ref, p_gate, q_gate, sems):
        core = core_of()

        def loads(first, second):
            return (
                pltpu.make_async_copy(first, p_gate, sems.at[0]),
                pltpu.make_async_copy(second, q_gate, sems.at[1]),
            )

        for number, refs in ((0, (query_ref, key_ref)), (1, (key_ref, query_ref))):

            @pl.when(core == number)
            def _():
                for load in loads(*refs):
                    load.start()

        for role, panels in enumerate(((p0, p1), (q0, q1))):
            for frame in range(2):
                for b in range(nb):
                    at = pl.ds(b * bw, bw)
                    out_ref[role, frame, :, at] = jnp.dot(
                        t_ref[role, frame * nb + b, 0], panels[frame][:, at], preferred_element_type=F32
                    )
        for load in loads(key_ref, query_ref):
            load.wait()

    gate = jax.ShapeDtypeStruct((span, 2 * hw), BF16)
    return call(
        body,
        "near_sums",
        [jax.ShapeDtypeStruct((2, 2, span, hw), F32), gate, gate],
        [VMEM] * 5 + [HBM] * 2,
        [VMEM] * 3,
        [pltpu.SemaphoreType.DMA((2,))],
    )(toeplitz, *p_own, *q_own, key, query)


def partial_sums(lags, slots, toeplitz, sums, r1, x2):
    span, hw = r1[0].shape
    bw = min(GSIZE, hw)
    nb = hw // bw

    def body(lag_ref, t_ref, sums_ref, r10, r11, x20, x21, out_ref):
        core = core_of()
        for frame in range(2):
            half = core if frame == 0 else 1 - core
            for b in range(nb):
                at = pl.ds(b * bw, bw)
                group = block_group(half, b, 2 * hw, bw)
                is_one = short_lag(lag_ref, group, slots) == 1
                panel = jnp.where(is_one, (r10, r11)[frame][:, at], (x20, x21)[frame][:, at])
                panel = kept(panel, jnp.where(is_one, valid("P", 1), valid("P", 2)))
                total = sums_ref[0, frame, :, at]
                total += jnp.dot(t_ref[0, frame * nb + b, 1], panel, preferred_element_type=F32)
                out_ref[frame, :, at] = total

    return call(
        body,
        "partial_sums",
        jax.ShapeDtypeStruct((2, span, hw), F32),
        [SMEM] + [VMEM] * 6,
        VMEM,
        flops=PARTIAL_SUMS_FLOPS,
    )(lags, toeplitz, sums, *r1, *x2)


def gated_output(role, frames, panels, total_of, gate, results, gradients=None):
    span, width = gate.shape
    hw = width // 2
    bw = min(GSIZE, hw)
    nb = hw // bw
    role_at = 0 if role == "P" else 1
    count = len(panels)
    lists, shapes, lay_out = gradients or ([], [], None)
    first = count + 1 + len(lists)

    def body(*refs):
        lag_ref, panel_refs, gate_ref = refs[0], refs[1:count], refs[count]
        row_refs = refs[count + 1 : count + 1 + len(lists)]
        outs = refs[first + len(results) :]
        block_ref, values_ref, grad_refs = outs[0], outs[1], outs[2 : 2 + len(shapes)]
        held, sems, grads_held = outs[2 + len(shapes)], outs[3 + len(shapes)], outs[4 + len(shapes) :]
        core = core_of()
        to_block = core == role_at

        def store(at, columns, ref):
            return pltpu.make_async_copy(held.at[at], ref.at[:, columns], sems.at[at])

        for at in range(len(frames) * nb):
            frame, b = frames[at // nb], at % nb
            half = core if frame == 0 else 1 - core
            group = block_group(half, b, width, bw)
            total = total_of(lag_ref, group, frame, frame * nb + b, pl.ds(b * bw, bw), *panel_refs)
            columns = pl.ds(pl.multiple_of(half * hw + b * bw, 128), bw)
            held[at] = (total * gate_ref[:, columns].astype(F32)).astype(BF16)

            @pl.when(to_block)
            def _():
                store(at, columns, block_ref).start()

            @pl.when(jnp.logical_not(to_block))
            def _():
                store(at, columns, values_ref).start()

        if shapes:
            lay_out(row_refs, grads_held)
        copies = [
            pltpu.make_async_copy(source, target, sems.at[len(frames) * nb + i])
            for i, (source, target) in enumerate(zip(grads_held, grad_refs))
        ]
        for copy in copies:
            copy.start()
        for at in range(len(frames) * nb):
            store(at, pl.ds(0, bw), block_ref).wait()
        for copy in copies:
            copy.wait()

    shape = jax.ShapeDtypeStruct((span, width), BF16)
    return call(
        body,
        f"out_{role.lower()}" + "".join(map(str, frames)),
        [shape, shape, *shapes],
        [SMEM] + [VMEM] * (count + len(lists)) + [HBM] * len(results),
        [HBM] * (2 + len(shapes)),
        [
            pltpu.VMEM((len(frames) * nb, span, bw), BF16),
            pltpu.SemaphoreType.DMA((len(frames) * nb + len(shapes),)),
            *[pltpu.VMEM(s.shape, s.dtype) for s in shapes],
        ],
        {first: 0, first + 1: 1} if results else None,
    )(*panels, gate, *lists, *results)


def q_output(frame, lags, slots, toeplitz, sums, x0, x1, r2, gate, results):
    def total_of(lag_ref, group, frame, place, at, t_ref, sums_ref, x0_ref, x1_ref, r2_ref):
        is_one = short_lag(lag_ref, group, slots) == 1
        panel = kept(jnp.where(is_one, x0_ref[:, at], x1_ref[:, at]), jnp.logical_or(is_one, valid("Q", 2)))
        last = kept(r2_ref[:, at], valid("Q", 3))
        total = sums_ref[1, frame, :, at]
        total += jnp.dot(t_ref[1, place, 1], panel, preferred_element_type=F32)
        return total + jnp.dot(t_ref[1, place, 2], last, preferred_element_type=F32)

    return gated_output("Q", (frame,), (lags, toeplitz, sums, x0, x1, r2), total_of, gate, results)


def p_output(lags, toeplitz, sums, r3, gate, results, gradients):
    def total_of(lag_ref, group, frame, place, at, t_ref, sums_ref, r3_ref):
        last = kept(r3_ref[frame, :, at], valid("P", 3))
        return sums_ref[frame, :, at] + jnp.dot(t_ref[0, place, 2], last, preferred_element_type=F32)

    return gated_output("P", (0, 1), (lags, toeplitz, sums, r3), total_of, gate, results, gradients)


def after(value, *others):
    return lax.optimization_barrier((value,) + others)[0]


def stacked(parts):
    def body(*refs):
        for i, ref in enumerate(refs[:-1]):
            refs[-1][i] = ref[...]

    shape = jax.ShapeDtypeStruct((len(parts),) + parts[0].shape, parts[0].dtype)
    return call(body, "stack", shape, [VMEM] * len(parts), VMEM)(*parts)


def added(parts):
    def body(*refs):
        terms = [ref[...] for ref in refs[:-1]]
        while len(terms) > 1:
            terms = [a + b for a, b in zip(terms[::2], terms[1::2])]
        refs[-1][...] = terms[0]

    shape = jax.ShapeDtypeStruct(parts[0].shape, F32)
    return call(body, "add_rows", shape, [VMEM] * len(parts), VMEM)(*parts)


def sum_over_chips(rows, work):
    count = lax.axis_size("ctx")
    if count & (count - 1):
        return lax.psum(rows, "ctx")
    bit = 2
    while bit < count:
        steps = [k * bit for k in (1, 2, 3) if k * bit < count]
        others = [lax.ppermute(rows, "ctx", [(i, i ^ step) for i in range(count)]) for step in steps]
        if bit == 2:
            others = list(lax.optimization_barrier((*others, work))[:-1])
        rows = added(others[::-1] + [rows])
        bit *= 4
    return rows


def sum_over_cores(rows):
    count = lax.axis_size("ctx")
    if count & (count - 1):
        return rows
    return added([rows, lax.ppermute(rows, "ctx", [(i, i ^ 1) for i in range(count)])])


def joined(first, second, bit):
    def body(first_ref, second_ref, out_ref):
        length = first_ref.shape[0]
        here = lax.rem(lax.div(lax.axis_index("chan"), bit), 2)
        out_ref[pl.ds(here * length, length)] = first_ref[...]
        out_ref[pl.ds((1 - here) * length, length)] = second_ref[...]

    shape = jax.ShapeDtypeStruct((2 * first.shape[0],) + first.shape[1:], F32)
    return call(body, "join_rows", shape, [VMEM] * 2, VMEM)(first, second)


def crossed(bit):
    ctxs, chans = lax.axis_size("ctx"), lax.axis_size("chan")
    core = 1 if ctxs % 2 == 0 else 0
    return [(i * chans + c, (i ^ core) * chans + (c ^ bit)) for i in range(ctxs) for c in range(chans)]


def gather_over_chan(rows, works):
    count = lax.axis_size("chan")
    if count & (count - 1):
        return lax.all_gather(rows, "chan", axis=0, tiled=True), None
    bit, other = 1, None
    while bit < count:
        if other is not None:
            rows = joined(rows, other, bit // 2)
        other = lax.ppermute(rows, ("ctx", "chan"), crossed(bit))
        if works:
            other = after(other, works[0])
            works = works[1:]
        bit *= 2
    return rows, other


def filter_gradients(rows, other, groups, span, scale):
    blocks, rows_per, doubled = rows.shape
    lists = [rows] if other is None else [rows, other]
    repeat = len(lists) * blocks // groups
    count = lax.axis_size("chan")

    def lay_out(refs, outs):
        far_ref, near_ref = outs
        upper = lax.div(2 * lax.axis_index("chan"), count) if len(lists) == 2 else 0
        for at in range(0, len(lists) * blocks, repeat):
            source = refs[at // blocks]
            total = source[at % blocks]
            for more in range(at % blocks + 1, at % blocks + repeat):
                total = total + source[more]
            place = at // repeat
            if len(lists) == 2:
                place = lax.rem(place + upper * (groups // 2), groups)
            far_ref[place] = total[1:] * scale
            near_ref[pl.ds(place, 1), :] = total[:1, span:] * scale

    shapes = [
        jax.ShapeDtypeStruct((groups, rows_per - 1, doubled), F32),
        jax.ShapeDtypeStruct((groups, span), F32),
    ]
    return lists, shapes, lay_out


def per_device(
    key_stream, value_stream, query_stream, grad_out, distant_lag_taps, near_taps, lag_blocks
):
    span, width = key_stream.shape
    groups = distant_lag_taps.shape[0]
    count = lax.axis_size("ctx")
    hw = width // 2
    bw = min(GSIZE, hw)

    def along(moves):
        chans = lax.axis_size("chan")
        moves = [(a, b) for a, b in moves if 0 <= b < count]
        sources, targets = {a for a, _ in moves}, {b for _, b in moves}
        moves += [(a, a ^ 1) for a in targets - sources if (a ^ 1) in sources - targets]
        pairs = [(a * chans + c, b * chans + c) for a, b in moves for c in range(chans)]
        if chans % 2 == 0:
            idle = set(range(count)) - sources - targets
            pairs += [(a * chans + c, a * chans + (c ^ 1)) for a in sorted(idle) for c in range(chans)]
        return sorted(pairs)

    swap = along([(i, i ^ 1) for i in range(count)])
    to_near = along([(i, i + 1 if i % 2 else i - 1) for i in range(count)])
    to_far = along([(i, i - 3 if i % 2 else i + 3) for i in range(count)])
    onward = along([(i, i - 2 if i % 2 else i + 2) for i in range(count)])

    def send(value, moves):
        return lax.ppermute(value, ("ctx", "chan"), moves)

    slots = lag_blocks.shape[1]
    streams = (key_stream, value_stream, query_stream, grad_out)
    streams = tuple(pltpu.with_memory_space_constraint(x, pltpu.HBM) for x in streams)
    qa, qb = stream_products(("Q0", "Q1"), streams, "q_stream")
    r1a, r1b = send(qa, to_near), send(qb, to_near)
    *late, far_taps, near_taps, lags, _ = lax.optimization_barrier(
        streams + (distant_lag_taps, near_taps, lag_blocks, qb)
    )
    lags = lags.reshape(-1)
    pa, pb = stream_products(("P0", "P1"), late, "p_stream")
    q_own, p_own = (qb, qa), (pb, pa)
    toeplitz = toeplitz_matrices(lags, far_taps, near_taps, span, width, bw)
    near = correlate_near(p_own, q_own)

    sums, p_gate, q_gate = near_sums(toeplitz, p_own, q_own, streams[0], streams[2])

    r2a = send(after(pa, near, sums), to_far)
    r1 = lax.optimization_barrier(((r1a, r1b), sums, near))[0]
    x1 = (send(r1[1], swap), send(r1[0], swap))
    x0a = send(after(pa, r1), swap)
    r2b = send(after(pb, r1), to_far)
    both, r1 = lax.optimization_barrier((stacked(r1), r1))
    rows = correlate_far(lags, slots, near, p_own, q_own, r1[0], x0a, x1, r2a)
    r3 = send(after(both, rows), onward)
    q_sums, pb_late, r2b, _ = lax.optimization_barrier((sums, pb, r2b, rows))
    results = q_output(0, lags, slots, toeplitz, q_sums, x0a, x1[0], r2a, q_gate, ())
    x0b = send(after(pb_late, r2b), swap)
    rows = sum_over_cores(sum_over_chips(rows, results[0]))
    r2_late, rows = lax.optimization_barrier(((r2a, r2b), rows))
    x2 = (send(r2_late[1], swap), send(r2_late[0], swap))
    results = q_output(1, lags, slots, toeplitz, sums, x0b, x1[1], r2b, q_gate, results)
    sums = partial_sums(lags, slots, toeplitz, sums, r1, x2)
    rows, other = gather_over_chan(rows, [results[0], sums])
    scale = 1.0 / math.sqrt(span * count * GSIZE)
    gradients = filter_gradients(rows, other, groups, span, scale)
    return tuple(p_output(lags, toeplitz, sums, r3, p_gate, results, gradients))


def solution(mesh):
    streams = P("ctx", "chan")
    return jax.shard_map(
        per_device,
        mesh=mesh,
        in_specs=(streams, streams, streams, streams, P(), P(), P()),
        out_specs=(streams, streams, P(), P()),
        check_vma=False,
    )
```

```python
import functools
import math

import jax
import jax.numpy as jnp
from jax import lax
from jax.experimental import pallas as pl
from jax.experimental.pallas import tpu as pltpu
from jax.sharding import PartitionSpec as P

GSIZE = 512
WIN = 4
PARTIAL_SUMS_FLOPS = 52 * 10**8
VMEM_LIMIT = 16 * 1024 * 1024
BF16 = jnp.bfloat16
F32 = jnp.float32

VMEM = pl.BlockSpec(memory_space=pltpu.VMEM)
SMEM = pl.BlockSpec(memory_space=pltpu.SMEM)
HBM = pl.BlockSpec(memory_space=pltpu.HBM)


def core_of():
    return lax.rem(lax.axis_index("ctx"), 2)


def call(body, name, out_shape, in_specs, out_specs, scratch=(), aliases=None, limit=VMEM_LIMIT, flops=1):
    def run(*args):
        moved = sum(a.size * a.dtype.itemsize for a in args + tuple(jax.tree.leaves(out_shape)))
        return pl.pallas_call(
            body,
            in_specs=in_specs,
            out_specs=out_specs,
            out_shape=out_shape,
            scratch_shapes=scratch,
            input_output_aliases=aliases or {},
            compiler_params=pltpu.CompilerParams(vmem_limit_bytes=limit),
            cost_estimate=pl.CostEstimate(flops=flops, bytes_accessed=moved, transcendentals=0),
            name=name,
        )(*args)

    return run


def valid(stream, lag):
    place = lax.axis_index("ctx")
    earlier, later = place >= lag, place + lag < lax.axis_size("ctx")
    return jnp.where(core_of() == (0 if stream == "P" else 1), earlier, later)


def kept(panel, exists):
    return jnp.where(exists, panel, jnp.zeros_like(panel))


def block_group(half, block, width, bw):
    first = lax.axis_index("chan") * width + half * (width // 2) + block * bw
    return lax.div(first, GSIZE)


def rolled(value, shift):
    shift %= value.shape[1]
    if shift % 128 == 0:
        return value if shift == 0 else jnp.concatenate([value[:, -shift:], value[:, :-shift]], axis=1)
    return pltpu.roll(value, shift, 1)


def skew(taps, span):
    width = 2 * span
    row = rolled(jnp.broadcast_to(taps, (8, width)), span)
    index = lax.broadcasted_iota(jnp.int32, (8, width), 0)
    for bit in (1, 2, 4):
        row = jnp.where((index & bit) != 0, rolled(row, bit), row)
    filled = 8
    while filled < span:
        row = jnp.concatenate([row, rolled(row, filled)], axis=0)
        filled *= 2
    return row[:, :span]


def diagonal_sums(matrix, span):
    width = 2 * span
    rows = jnp.concatenate([matrix, jnp.zeros((span, span), F32)], axis=1)
    half = span // 2
    while half >= 8:
        rows = rows[:half] + rolled(rows[half:], -half)
        half //= 2
    index = lax.broadcasted_iota(jnp.int32, (8, width), 0)
    for bit in (1, 2, 4):
        rows = jnp.where((index & bit) != 0, rolled(rows, -bit), rows)
    return rolled(jnp.sum(rows, axis=0, keepdims=True), span)


def stream_products(wanted, streams, name):
    span, width = streams[0].shape
    hw = width // 2
    count = len(wanted)

    def body(k_ref, v_ref, q_ref, g_ref, *rest):
        outs, (held, sems) = rest[:-2], rest[-2:]
        core = core_of()

        def copies(at, pair):
            half = 1 - core if wanted[at][1] == "0" else core
            columns = pl.ds(pl.multiple_of(half * hw, 128), hw)
            return [
                pltpu.make_async_copy(ref.at[:, columns], held.at[at, i], sems.at[at, i])
                for i, ref in enumerate(pair)
            ]

        for at, kind in enumerate(wanted):
            mixed_core = 0 if kind[0] == "P" else 1
            for is_mixed, pair in ((True, (k_ref, v_ref)), (False, (g_ref, q_ref))):

                @pl.when((core == mixed_core) == is_mixed)
                def _():
                    for copy in copies(at, pair):
                        copy.start()

        for at in range(count):
            for copy in copies(at, (k_ref, v_ref)):
                copy.wait()
            product = (held[at, 0].astype(F32) * held[at, 1].astype(F32)).astype(BF16)
            outs[at][...] = product

    return call(
        body,
        name,
        [jax.ShapeDtypeStruct((span, hw), BF16)] * count,
        [HBM] * 4,
        [VMEM] * count,
        [pltpu.VMEM((count, 2, span, hw), BF16), pltpu.SemaphoreType.DMA((count, 2))],
    )(*streams)


def short_lag(lag_ref, group, slots):
    lag = lag_ref[group * slots]
    for slot in range(1, slots):
        lag = jnp.minimum(lag, lag_ref[group * slots + slot])
    return lag


def toeplitz_matrices(lags, far_taps, near_taps, span, width, bw):
    groups, slots, doubled = far_taps.shape
    nb = width // 2 // bw

    def body(lag_ref, far_ref, near_ref, out_ref, near_rows):
        core = core_of()
        near_rows[...] = near_ref[...].astype(F32)
        for frame in range(2):
            half = core if frame == 0 else 1 - core
            for b in range(nb):
                group = block_group(half, b, width, bw)
                far = far_ref[group].astype(F32)
                near = near_rows[pl.ds(group, 1), :]
                short = last = jnp.zeros((1, doubled), F32)
                for slot in range(slots):
                    is_last = lag_ref[group * slots + slot] == WIN - 1
                    taps = far[slot : slot + 1]
                    short = jnp.where(is_last, short, taps)
                    last = jnp.where(is_last, taps, last)
                near = jnp.concatenate([jnp.zeros((1, span), F32), near], axis=1)
                for at, taps in enumerate((near, short, last)):
                    matrix = skew(taps, span)
                    out_ref[1 - core, frame * nb + b, at] = matrix.astype(BF16)
                    out_ref[core, frame * nb + b, at] = matrix.T.astype(BF16)

    return call(
        body,
        "toeplitz",
        jax.ShapeDtypeStruct((2, 2 * nb, 3, span, span), BF16),
        [SMEM, VMEM, VMEM],
        VMEM,
        [pltpu.VMEM((groups, span), F32)],
    )(lags, far_taps, near_taps)


def outer(mixed, gated):
    return lax.dot_general(mixed, gated, (((1,), (1,)), ((), ())), preferred_element_type=F32)


def by_core(body):
    core = core_of()

    @pl.when(core == 0)
    def _():
        body(outer)

    @pl.when(core != 0)
    def _():
        body(lambda p, q: outer(q, p))


def correlate_near(p_own, q_own):
    span, hw = p_own[0].shape
    bw = min(GSIZE, hw)
    nb = hw // bw

    def body(p0, p1, q0, q1, rows_ref):
        def run(pair):
            for frame in range(2):
                for b in range(nb):
                    at = pl.ds(b * bw, bw)
                    matrix = pair((p0, p1)[frame][:, at], (q0, q1)[frame][:, at])
                    rows_ref[frame, pl.ds(b, 1), :] = diagonal_sums(matrix, span)

        by_core(run)

    return call(
        body,
        "correlate_near",
        jax.ShapeDtypeStruct((2, nb, 2 * span), F32),
        [VMEM] * 4,
        VMEM,
    )(*p_own, *q_own)


def correlate_first(lags, slots, q_own, r1):
    span, hw = r1.shape
    bw = min(GSIZE, hw)
    nb = hw // bw

    def body(lag_ref, q_ref, r1_ref, out_ref):
        core = core_of()

        def run(pair):
            for b in range(nb):
                at = pl.ds(b * bw, bw)
                is_one = short_lag(lag_ref, block_group(core, b, 2 * hw, bw), slots) == 1
                used = jnp.logical_and(is_one, valid("P", 1))
                out_ref[b] = pair(kept(r1_ref[:, at], used), q_ref[:, at])

        by_core(run)

    return call(
        body,
        "correlate_first",
        jax.ShapeDtypeStruct((nb, span, span), F32),
        [SMEM] + [VMEM] * 2,
        VMEM,
    )(lags, q_own, r1)


def correlate_far(lags, slots, near, first, p_own, r1, x0, x1, r2):
    span, hw = r2.shape
    bw = min(GSIZE, hw)
    nb = hw // bw

    def body(lag_ref, near_ref, first_ref, p0, p1, r1_ref, x0_ref, x10, x11, r2_ref, out_ref):
        core = core_of()

        def run(pair):
            for b in range(nb):
                at = pl.ds(b * bw, bw)
                p, x, r = p0[:, at], kept(x10[:, at], valid("Q", 2)), kept(r1_ref[:, at], valid("P", 1))
                is_one = short_lag(lag_ref, block_group(core, b, 2 * hw, bw), slots) == 1
                short = first_ref[b] + pair(p, jnp.where(is_one, x0_ref[:, at], x))
                last = pair(r, x) + pair(p, kept(r2_ref[:, at], valid("Q", 3)))
                other = pair(p1[:, at], kept(x11[:, at], valid("Q", 2)))
                rows = [diagonal_sums(matrix, span) for matrix in (short, last, other)]
                empty = jnp.zeros_like(rows[0])
                for frame in range(2):
                    half = core if frame == 0 else 1 - core
                    group = block_group(half, b, 2 * hw, bw)
                    place = half * nb + b
                    if frame == 0:
                        close, distant = rows[0], rows[1]
                    else:
                        close = jnp.where(short_lag(lag_ref, group, slots) == 2, rows[2], empty)
                        distant = empty
                    out_ref[place, pl.ds(0, 1), :] = near_ref[frame, pl.ds(b, 1), :]
                    for slot in range(slots):
                        is_last = lag_ref[group * slots + slot] == WIN - 1
                        out_ref[place, pl.ds(1 + slot, 1), :] = jnp.where(is_last, distant, close)

        by_core(run)

    return call(
        body,
        "correlate_far",
        jax.ShapeDtypeStruct((2 * nb, slots + 1, 2 * span), F32),
        [SMEM] + [VMEM] * 9,
        VMEM,
    )(lags, near, first, *p_own, r1, x0, *x1, r2)


def near_sums(toeplitz, p_own, q_own, key, query):
    span, hw = p_own[0].shape
    bw = min(GSIZE, hw)
    nb = hw // bw

    def body(t_ref, p0, p1, q0, q1, key_ref, query_ref, out_ref, p_gate, q_gate, sems):
        core = core_of()

        def loads(first, second):
            return (
                pltpu.make_async_copy(first, p_gate, sems.at[0]),
                pltpu.make_async_copy(second, q_gate, sems.at[1]),
            )

        for number, refs in ((0, (query_ref, key_ref)), (1, (key_ref, query_ref))):

            @pl.when(core == number)
            def _():
                for load in loads(*refs):
                    load.start()

        for role, panels in enumerate(((p0, p1), (q0, q1))):
            for frame in range(2):
                for b in range(nb):
                    at = pl.ds(b * bw, bw)
                    out_ref[role, frame, :, at] = jnp.dot(
                        t_ref[role, frame * nb + b, 0], panels[frame][:, at], preferred_element_type=F32
                    )
        for load in loads(key_ref, query_ref):
            load.wait()

    gate = jax.ShapeDtypeStruct((span, 2 * hw), BF16)
    return call(
        body,
        "near_sums",
        [jax.ShapeDtypeStruct((2, 2, span, hw), F32), gate, gate],
        [VMEM] * 5 + [HBM] * 2,
        [VMEM] * 3,
        [pltpu.SemaphoreType.DMA((2,))],
    )(toeplitz, *p_own, *q_own, key, query)


def partial_sums(lags, slots, toeplitz, sums, r1, x2):
    span, hw = r1[0].shape
    bw = min(GSIZE, hw)
    nb = hw // bw

    def body(lag_ref, t_ref, sums_ref, r10, r11, x20, x21, out_ref):
        core = core_of()
        for frame in range(2):
            half = core if frame == 0 else 1 - core
            for b in range(nb):
                at = pl.ds(b * bw, bw)
                group = block_group(half, b, 2 * hw, bw)
                is_one = short_lag(lag_ref, group, slots) == 1
                panel = jnp.where(is_one, (r10, r11)[frame][:, at], (x20, x21)[frame][:, at])
                panel = kept(panel, jnp.where(is_one, valid("P", 1), valid("P", 2)))
                total = sums_ref[0, frame, :, at]
                total += jnp.dot(t_ref[0, frame * nb + b, 1], panel, preferred_element_type=F32)
                out_ref[frame, :, at] = total

    return call(
        body,
        "partial_sums",
        jax.ShapeDtypeStruct((2, span, hw), F32),
        [SMEM] + [VMEM] * 6,
        VMEM,
        flops=PARTIAL_SUMS_FLOPS,
    )(lags, toeplitz, sums, *r1, *x2)


def gated_output(role, frames, panels, total_of, gate, results, gradients=None):
    span, width = gate.shape
    hw = width // 2
    bw = min(GSIZE, hw)
    nb = hw // bw
    role_at = 0 if role == "P" else 1
    count = len(panels)
    lists, shapes, lay_out = gradients or ([], [], None)
    first = count + 1 + len(lists)

    def body(*refs):
        lag_ref, panel_refs, gate_ref = refs[0], refs[1:count], refs[count]
        row_refs = refs[count + 1 : count + 1 + len(lists)]
        outs = refs[first + len(results) :]
        block_ref, values_ref, grad_refs = outs[0], outs[1], outs[2 : 2 + len(shapes)]
        held, sems, grads_held = outs[2 + len(shapes)], outs[3 + len(shapes)], outs[4 + len(shapes) :]
        core = core_of()
        to_block = core == role_at

        def store(at, columns, ref):
            return pltpu.make_async_copy(held.at[at], ref.at[:, columns], sems.at[at])

        for at in range(len(frames) * nb):
            frame, b = frames[at // nb], at % nb
            half = core if frame == 0 else 1 - core
            group = block_group(half, b, width, bw)
            total = total_of(lag_ref, group, frame, frame * nb + b, pl.ds(b * bw, bw), *panel_refs)
            columns = pl.ds(pl.multiple_of(half * hw + b * bw, 128), bw)
            held[at] = (total * gate_ref[:, columns].astype(F32)).astype(BF16)

            @pl.when(to_block)
            def _():
                store(at, columns, block_ref).start()

            @pl.when(jnp.logical_not(to_block))
            def _():
                store(at, columns, values_ref).start()

        if shapes:
            lay_out(row_refs, grads_held)
        copies = [
            pltpu.make_async_copy(source, target, sems.at[len(frames) * nb + i])
            for i, (source, target) in enumerate(zip(grads_held, grad_refs))
        ]
        for copy in copies:
            copy.start()
        for at in range(len(frames) * nb):
            store(at, pl.ds(0, bw), block_ref).wait()
        for copy in copies:
            copy.wait()

    shape = jax.ShapeDtypeStruct((span, width), BF16)
    return call(
        body,
        f"out_{role.lower()}" + "".join(map(str, frames)),
        [shape, shape, *shapes],
        [SMEM] + [VMEM] * (count + len(lists)) + [HBM] * len(results),
        [HBM] * (2 + len(shapes)),
        [
            pltpu.VMEM((len(frames) * nb, span, bw), BF16),
            pltpu.SemaphoreType.DMA((len(frames) * nb + len(shapes),)),
            *[pltpu.VMEM(s.shape, s.dtype) for s in shapes],
        ],
        {first: 0, first + 1: 1} if results else None,
    )(*panels, gate, *lists, *results)


def q_output(frame, lags, slots, toeplitz, sums, x0, x1, r2, gate, results):
    def total_of(lag_ref, group, frame, place, at, t_ref, sums_ref, x0_ref, x1_ref, r2_ref):
        is_one = short_lag(lag_ref, group, slots) == 1
        panel = kept(jnp.where(is_one, x0_ref[:, at], x1_ref[:, at]), jnp.logical_or(is_one, valid("Q", 2)))
        last = kept(r2_ref[:, at], valid("Q", 3))
        total = sums_ref[1, frame, :, at]
        total += jnp.dot(t_ref[1, place, 1], panel, preferred_element_type=F32)
        return total + jnp.dot(t_ref[1, place, 2], last, preferred_element_type=F32)

    return gated_output("Q", (frame,), (lags, toeplitz, sums, x0, x1, r2), total_of, gate, results)


def p_output(lags, toeplitz, sums, r3, gate, results, gradients):
    def total_of(lag_ref, group, frame, place, at, t_ref, sums_ref, r3_ref):
        last = kept(r3_ref[frame, :, at], valid("P", 3))
        return sums_ref[frame, :, at] + jnp.dot(t_ref[0, place, 2], last, preferred_element_type=F32)

    return gated_output("P", (0, 1), (lags, toeplitz, sums, r3), total_of, gate, results, gradients)


def after(value, *others):
    return lax.optimization_barrier((value,) + others)[0]


def stacked(parts):
    def body(*refs):
        for i, ref in enumerate(refs[:-1]):
            refs[-1][i] = ref[...]

    shape = jax.ShapeDtypeStruct((len(parts),) + parts[0].shape, parts[0].dtype)
    return call(body, "stack", shape, [VMEM] * len(parts), VMEM)(*parts)


def added(parts):
    def body(*refs):
        terms = [ref[...] for ref in refs[:-1]]
        while len(terms) > 1:
            terms = [a + b for a, b in zip(terms[::2], terms[1::2])]
        refs[-1][...] = terms[0]

    shape = jax.ShapeDtypeStruct(parts[0].shape, F32)
    return call(body, "add_rows", shape, [VMEM] * len(parts), VMEM)(*parts)


def sum_over_chips(rows, work):
    count = lax.axis_size("ctx")
    if count & (count - 1):
        return lax.psum(rows, "ctx")
    bit = 2
    while bit < count:
        steps = [k * bit for k in (1, 2, 3) if k * bit < count]
        others = [lax.ppermute(rows, "ctx", [(i, i ^ step) for i in range(count)]) for step in steps]
        if bit == 2:
            others = list(lax.optimization_barrier((*others, work))[:-1])
        rows = added(others[::-1] + [rows])
        bit *= 4
    return rows


def sum_over_cores(rows):
    count = lax.axis_size("ctx")
    if count & (count - 1):
        return rows
    return added([rows, lax.ppermute(rows, "ctx", [(i, i ^ 1) for i in range(count)])])


def joined(first, second, bit):
    def body(first_ref, second_ref, out_ref):
        length = first_ref.shape[0]
        here = lax.rem(lax.div(lax.axis_index("chan"), bit), 2)
        out_ref[pl.ds(here * length, length)] = first_ref[...]
        out_ref[pl.ds((1 - here) * length, length)] = second_ref[...]

    shape = jax.ShapeDtypeStruct((2 * first.shape[0],) + first.shape[1:], F32)
    return call(body, "join_rows", shape, [VMEM] * 2, VMEM)(first, second)


def crossed(bit):
    ctxs, chans = lax.axis_size("ctx"), lax.axis_size("chan")
    core = 1 if ctxs % 2 == 0 else 0
    return [(i * chans + c, (i ^ core) * chans + (c ^ bit)) for i in range(ctxs) for c in range(chans)]


def gather_over_chan(rows, works):
    count = lax.axis_size("chan")
    if count & (count - 1):
        return lax.all_gather(rows, "chan", axis=0, tiled=True), None
    bit, other = 1, None
    while bit < count:
        if other is not None:
            rows = joined(rows, other, bit // 2)
        other = lax.ppermute(rows, ("ctx", "chan"), crossed(bit))
        if works:
            other = after(other, works[0])
            works = works[1:]
        bit *= 2
    return rows, other


def filter_gradients(rows, other, groups, span, scale):
    blocks, rows_per, doubled = rows.shape
    lists = [rows] if other is None else [rows, other]
    repeat = len(lists) * blocks // groups
    count = lax.axis_size("chan")

    def lay_out(refs, outs):
        far_ref, near_ref = outs
        upper = lax.div(2 * lax.axis_index("chan"), count) if len(lists) == 2 else 0
        for at in range(0, len(lists) * blocks, repeat):
            source = refs[at // blocks]
            total = source[at % blocks]
            for more in range(at % blocks + 1, at % blocks + repeat):
                total = total + source[more]
            place = at // repeat
            if len(lists) == 2:
                place = lax.rem(place + upper * (groups // 2), groups)
            far_ref[place] = total[1:] * scale
            near_ref[pl.ds(place, 1), :] = total[:1, span:] * scale

    shapes = [
        jax.ShapeDtypeStruct((groups, rows_per - 1, doubled), F32),
        jax.ShapeDtypeStruct((groups, span), F32),
    ]
    return lists, shapes, lay_out


def per_device(
    key_stream, value_stream, query_stream, grad_out, distant_lag_taps, near_taps, lag_blocks
):
    span, width = key_stream.shape
    groups = distant_lag_taps.shape[0]
    count = lax.axis_size("ctx")
    hw = width // 2
    bw = min(GSIZE, hw)

    def along(moves):
        chans = lax.axis_size("chan")
        moves = [(a, b) for a, b in moves if 0 <= b < count]
        sources, targets = {a for a, _ in moves}, {b for _, b in moves}
        moves += [(a, a ^ 1) for a in targets - sources if (a ^ 1) in sources - targets]
        pairs = [(a * chans + c, b * chans + c) for a, b in moves for c in range(chans)]
        if chans % 2 == 0:
            idle = set(range(count)) - sources - targets
            pairs += [(a * chans + c, a * chans + (c ^ 1)) for a in sorted(idle) for c in range(chans)]
        return sorted(pairs)

    swap = along([(i, i ^ 1) for i in range(count)])
    to_near = along([(i, i + 1 if i % 2 else i - 1) for i in range(count)])
    to_far = along([(i, i - 3 if i % 2 else i + 3) for i in range(count)])
    onward = along([(i, i - 2 if i % 2 else i + 2) for i in range(count)])

    def send(value, moves):
        return lax.ppermute(value, ("ctx", "chan"), moves)

    slots = lag_blocks.shape[1]
    streams = (key_stream, value_stream, query_stream, grad_out)
    streams = tuple(pltpu.with_memory_space_constraint(x, pltpu.HBM) for x in streams)
    qa, qb = stream_products(("Q0", "Q1"), streams, "q_stream")
    r1a, r1b = send(qa, to_near), send(qb, to_near)
    *late, far_taps, near_taps, lags, _ = lax.optimization_barrier(
        streams + (distant_lag_taps, near_taps, lag_blocks, qb)
    )
    lags = lags.reshape(-1)
    pa, pb = stream_products(("P0", "P1"), late, "p_stream")
    q_own, p_own = (qb, qa), (pb, pa)
    toeplitz = toeplitz_matrices(lags, far_taps, near_taps, span, width, bw)
    near = correlate_near(p_own, q_own)

    sums, p_gate, q_gate = near_sums(toeplitz, p_own, q_own, streams[0], streams[2])

    r2a = send(after(pa, near, sums), to_far)
    r1 = lax.optimization_barrier(((r1a, r1b), sums, near))[0]
    x1 = (send(r1[1], swap), send(r1[0], swap))
    x0a = send(after(pa, r1), swap)
    r2b = send(after(pb, r1), to_far)
    first = correlate_first(lags, slots, q_own[0], r1[0])
    both, first, r1 = lax.optimization_barrier((stacked(r1), first, r1))
    rows = correlate_far(lags, slots, near, first, p_own, r1[0], x0a, x1, r2a)
    r3 = send(after(both, rows), onward)
    q_sums, pb_late, r2b, _ = lax.optimization_barrier((sums, pb, r2b, rows))
    results = q_output(0, lags, slots, toeplitz, q_sums, x0a, x1[0], r2a, q_gate, ())
    x0b = send(after(pb_late, r2b), swap)
    rows = sum_over_cores(sum_over_chips(rows, results[0]))
    r2_late, rows = lax.optimization_barrier(((r2a, r2b), rows))
    x2 = (send(r2_late[1], swap), send(r2_late[0], swap))
    results = q_output(1, lags, slots, toeplitz, sums, x0b, x1[1], r2b, q_gate, results)
    sums = partial_sums(lags, slots, toeplitz, sums, r1, x2)
    rows, other = gather_over_chan(rows, [results[0], sums])
    scale = 1.0 / math.sqrt(span * count * GSIZE)
    gradients = filter_gradients(rows, other, groups, span, scale)
    return tuple(p_output(lags, toeplitz, sums, r3, p_gate, results, gradients))


def solution(mesh):
    streams = P("ctx", "chan")
    return jax.shard_map(
        per_device,
        mesh=mesh,
        in_specs=(streams, streams, streams, streams, P(), P(), P()),
        out_specs=(streams, streams, P(), P()),
        check_vma=False,
    )
```
